32 devices in a mesh: dp: 16 (over z, x, core), ctx: 2 (over y).
Axes of the slice: x: 2, y: 2, z: 4, core: 2. Of those that a mesh axis runs over, the one named last changes fastest.
Arguments:
- clip_in: bfloat16 [16, 8, 4, 96, 128], P('dp', 'ctx'), may hold values from -100 to 100
- norm_gain: float32 [128], replicated, may hold values from 0.1 to 1.9
- norm_bias: float32 [128], replicated, may hold values from -3 to 3
- conv_weight: bfloat16 [3456, 256], replicated, may hold values from -0.109375 to 0.109375
- short_weight: bfloat16 [128, 256], replicated, may hold values from -0.5 to 0.5
- out_cotangent: bfloat16 [16, 8, 4, 96, 256], P('dp', 'ctx'), may hold values from -6 to 6
Outputs:
- clip_out: bfloat16 [16, 8, 4, 96, 256], P('dp', 'ctx')
- clip_grad: bfloat16 [16, 8, 4, 96, 128], P('dp', 'ctx')
- conv_grad: float32 [3456, 256], P('dp', 'ctx')
- short_grad: float32 [128, 256], P('dp', 'ctx')
The draws below stay inside these ranges and needn't reach their ends.
All inputs are finite; a program needn't handle non-finite values.
Results may differ from the reference program's by a relative error of at most 0.0027.
Values may be sent and summed in bfloat16 or wider, within the bound.
No kernel may reach another device: no remote copies, remote signals or barrier semaphores. Data moves between devices by JAX's collectives and lax.ppermute only.
A program may use at most 128 MiB of HBM per device.

```python
import math
import jax
import jax.numpy as jnp
from jax import lax

CIN = 128
COUT = 256
GROUPS = 32
KT = 3
KS = 3
ROWS = 4
COLS = 96
CLIPS = 16
FRAMES = 8


def draw_clip_in(key, part):
    key_base, key_chan, key_rows, key_offset = jax.random.split(key, 4)
    extent = (CLIPS, FRAMES, ROWS, COLS, CIN)
    channel_scale = jnp.exp(jax.random.uniform(key_chan, (CIN,), jnp.float32, math.log(0.3), math.log(3.0)))
    row_scale = jnp.exp(jax.random.uniform(key_rows, (CLIPS, FRAMES, ROWS, 1, 1), jnp.float32, math.log(0.5), math.log(2.0)))
    frame_ramp = jnp.exp(math.log(3.0) * jnp.arange(FRAMES, dtype=jnp.float32) / max(FRAMES - 1, 1)).reshape(1, FRAMES, 1, 1, 1)
    base_vals = jnp.clip(jax.random.normal(key_base, extent, jnp.float32), -4.0, 4.0)
    offset_vals = 0.3 * jnp.clip(jax.random.normal(key_offset, (CLIPS, 1, 1, 1, CIN), jnp.float32), -3.0, 3.0)
    return ((base_vals * channel_scale + offset_vals) * row_scale * frame_ramp).astype(jnp.bfloat16)


def with_spikes(entries, stream_key, source, target, parts, factor):
    def block_of(axis_at):
        return (jnp.arange(entries.shape[axis_at]) // (entries.shape[axis_at] // parts)).reshape((-1,) + (1,) * (entries.ndim - 1 - axis_at))

    near = jax.random.permutation(stream_key, parts)[block_of(target)]
    other_side = (block_of(target) + parts // 2) % parts
    return jnp.where((block_of(source) == near) | (block_of(source) == other_side), factor * entries, entries)


def block_scale(rng, dims, cuts, low, high):
    gain, own = 1.0, jax.random.fold_in(rng, 6)
    for axis_at, parts in cuts:
        heights = jnp.exp(jax.random.uniform(jax.random.fold_in(own, axis_at), (parts,), jnp.float32, low / len(cuts), high / len(cuts)))
        gain = gain * jnp.repeat(heights, dims[axis_at] // parts).reshape([-1 if axis == axis_at else 1 for axis in range(len(dims))])
    return gain


def normal_values(own_key, shape, deviation, bound, shards=(), held_as=jnp.bfloat16):
    values = jax.random.normal(own_key, shape, jnp.float32) * deviation
    if len(shards) > 0:
        values = block_scale(own_key, shape, shards, -0.22, 0.18) * values
    return jnp.clip(values, min=-bound, max=bound).astype(held_as)


def gaussian_with(stream_key, shape, width, bound, cuts, heavy, kind=jnp.bfloat16):
    values = width * jax.random.normal(stream_key, shape, jnp.float32)
    if cuts:
        values = values * block_scale(stream_key, shape, cuts, -0.22, 0.18)
    return jnp.clip(with_spikes(values, jax.random.fold_in(stream_key, 3), *heavy), -bound, bound).astype(kind)


def setup_inputs(seed: int = 0) -> dict:
    arg_keys = jax.random.split(jax.random.key(seed), 7)
    clip_in = draw_clip_in(jax.random.fold_in(arg_keys[6], 71), 0)
    norm_gain = jnp.clip(1.0 + 0.18 * jax.random.normal(arg_keys[1], (CIN,), jnp.float32), 0.1, 1.9)
    norm_bias = normal_values(arg_keys[2], (CIN,), 0.5, 3.0, (), jnp.float32)
    conv_weight = normal_values(arg_keys[3], (KT * KS * KS * CIN, COUT), (KT * KS * KS * CIN) ** -0.5, 0.109375)
    short_weight = normal_values(arg_keys[4], (CIN, COUT), CIN ** -0.5, 0.5)
    out_cotangent = gaussian_with(arg_keys[5], (CLIPS, FRAMES, ROWS, COLS, COUT), 1.0, 6.0, ((0, 16), (1, 2)), (0, 4, 16, 2.0))
    return {"clip_in": clip_in, "norm_gain": norm_gain, "norm_bias": norm_bias, "conv_weight": conv_weight, "short_weight": short_weight, "out_cotangent": out_cotangent}


epsilon = 1e-06

def reference(clip_in, norm_gain, norm_bias, conv_weight, short_weight, out_cotangent):
    per_group = CIN // GROUPS
    members = FRAMES * ROWS * COLS * per_group
    w_back = conv_weight.reshape(KT, KS * KS, CIN, COUT).transpose(0, 1, 3, 2).reshape(KT, KS * KS * COUT, CIN)

    def one_clip(inputs):
        clip_vals, clip_cot = inputs
        widened = clip_vals.astype(jnp.float32)
        grouped = widened.reshape(FRAMES, ROWS, COLS, GROUPS, per_group)
        group_mean = lax.optimization_barrier(jnp.sum(grouped, axis=(0, 1, 2, 4))) / members
        variance = lax.optimization_barrier(jnp.sum(grouped * grouped, axis=(0, 1, 2, 4))) / members - group_mean * group_mean
        inv_std = lax.rsqrt(variance + epsilon)
        mean_chan = jnp.repeat(group_mean, per_group)
        inv_chan = jnp.repeat(inv_std, per_group)
        standard = (widened - mean_chan) * inv_chan
        affine = standard * norm_gain + norm_bias
        hidden = jax.nn.silu(affine).astype(jnp.bfloat16)
        padded = jnp.concatenate([hidden[:1], hidden[:1], hidden], axis=0)
        padded = jnp.pad(padded, ((0, 0), (1, 1), (1, 1), (0, 0)))
        pieces = []
        for tap_t in range(KT):
            for tap_r in range(KS):
                for tap_c in range(KS):
                    pieces.append(padded[tap_t:tap_t + FRAMES, tap_r:tap_r + ROWS, tap_c:tap_c + COLS])
        columns = jnp.concatenate(pieces, axis=-1).reshape(-1, KT * KS * KS * CIN)
        cot_flat = clip_cot.reshape(-1, COUT)
        in_flat = clip_vals.reshape(-1, CIN)
        result = jnp.dot(columns, conv_weight, preferred_element_type=jnp.float32)
        result = result + jnp.dot(in_flat, short_weight, preferred_element_type=jnp.float32)
        result = result.astype(jnp.bfloat16).reshape(FRAMES, ROWS, COLS, COUT)
        conv_part = lax.dot_general(columns, cot_flat, (((0,), (0,)), ((), ())), preferred_element_type=jnp.float32)
        short_part = lax.dot_general(in_flat, cot_flat, (((0,), (0,)), ((), ())), preferred_element_type=jnp.float32)
        padded_cot = jnp.pad(clip_cot, ((2, 2), (1, 1), (1, 1), (0, 0)))
        spatial = []
        for tap_r in range(KS):
            for tap_c in range(KS):
                spatial.append(padded_cot[:, 2 - tap_r:2 - tap_r + ROWS, 2 - tap_c:2 - tap_c + COLS])
        spatial = jnp.concatenate(spatial, axis=-1)
        back_all = jnp.zeros(((FRAMES + 2) * ROWS * COLS, CIN), jnp.float32)
        for tap_t in range(KT):
            block = spatial[2 - tap_t:2 - tap_t + FRAMES + 2].reshape(-1, KS * KS * COUT)
            back_all = back_all + jnp.dot(block, w_back[tap_t], preferred_element_type=jnp.float32)
        back_all = back_all.reshape(FRAMES + 2, ROWS, COLS, CIN)
        grad_hidden = back_all[2:]
        grad_hidden = grad_hidden.at[0].add(back_all[0] + back_all[1])
        logistic = jax.nn.sigmoid(affine)
        grad_standard = grad_hidden * logistic * (1.0 + affine * (1.0 - logistic)) * norm_gain
        grouped_grad = grad_standard.reshape(FRAMES, ROWS, COLS, GROUPS, per_group)
        grouped_std = standard.reshape(FRAMES, ROWS, COLS, GROUPS, per_group)
        mean_grad = jnp.repeat(lax.optimization_barrier(jnp.sum(grouped_grad, axis=(0, 1, 2, 4))) / members, per_group)
        mean_cross = jnp.repeat(lax.optimization_barrier(jnp.sum(grouped_grad * grouped_std, axis=(0, 1, 2, 4))) / members, per_group)
        shortcut = lax.dot_general(cot_flat, short_weight, (((1,), (1,)), ((), ())), preferred_element_type=jnp.float32)
        in_grad = (grad_standard - mean_grad - standard * mean_cross) * inv_chan + shortcut.reshape(FRAMES, ROWS, COLS, CIN)
        return (result, in_grad.astype(jnp.bfloat16), conv_part, short_part)
    clip_out, clip_grad, conv_parts, short_parts = lax.map(one_clip, (clip_in, out_cotangent))
    scale_factor = 1.0 / (CLIPS * FRAMES)
    conv_grad = lax.optimization_barrier(jnp.sum(conv_parts, axis=0)) * scale_factor
    short_grad = lax.optimization_barrier(jnp.sum(short_parts, axis=0)) * scale_factor
    return (clip_out, clip_grad, conv_grad, short_grad)
```

```python
import functools
import math

import jax
import jax.numpy as jnp
from jax import lax
from jax.experimental import pallas as pl
from jax.experimental.pallas import tpu as pltpu
from jax.sharding import PartitionSpec as P

GROUPS = 32
KT = 3
KS = 3
TAPS = KT * KS * KS
VMEM_BYTES = 48 * 1024 * 1024

epsilon = 1e-06
f32 = jnp.float32
bf16 = jnp.bfloat16


def call(kernel, outs, scratch=(), flops=0, moved=0):
    return pl.pallas_call(
        kernel,
        out_shape=outs,
        scratch_shapes=list(scratch),
        compiler_params=pltpu.CompilerParams(vmem_limit_bytes=VMEM_BYTES),
        cost_estimate=pl.CostEstimate(flops=flops, bytes_accessed=moved, transcendentals=0),
    )


def group_totals(rows):
    width = rows.shape[1]
    per_group = width // GROUPS
    row = lax.broadcasted_iota(jnp.int32, (width, width), 0) // per_group
    col = lax.broadcasted_iota(jnp.int32, (width, width), 1) // per_group
    same = (row == col).astype(f32)
    return lax.dot_general(
        rows, same, (((1,), (0,)), ((), ())), precision=lax.Precision.HIGHEST, preferred_element_type=f32
    )


def two_rows(first, second):
    at = lax.broadcasted_iota(jnp.int32, (8, first.shape[1]), 0)
    return jnp.where(at == 0, first, jnp.where(at == 1, second, 0.0))


def column_totals(value):
    return jnp.sum(value, axis=0, keepdims=True)


def stats_kernel(clip_ref, out_ref):
    frames = clip_ref.shape[0]
    width = clip_ref.shape[-1]
    total = jnp.zeros((1, width), f32)
    square = jnp.zeros((1, width), f32)
    for frame in range(frames):
        value = clip_ref[frame].reshape(-1, width).astype(f32)
        total = total + column_totals(value)
        square = square + column_totals(value * value)
    out_ref[...] = group_totals(two_rows(total, square))


def moments(stats_a, stats_b, members):
    totals = stats_a[...] + stats_b[...]
    mean = totals[0:1] / members
    variance = totals[1:2] / members - mean * mean
    return mean, lax.rsqrt(variance + epsilon)


def shift_columns(value, step):
    rows, cols, width = value.shape
    flat = value.reshape(rows * cols, width)
    rolled = pltpu.roll(flat, (-step) % (rows * cols), 0).reshape(rows, cols, width)
    at = lax.broadcasted_iota(jnp.int32, (rows, cols, width), 1)
    edge = cols - 1 if step == 1 else 0
    return jnp.where(at == edge, 0.0, rolled)


def place(padded, frame, value):
    rows, cols, width = value.shape
    for j, step in enumerate((-1, 0, 1)):
        moved = value if step == 0 else shift_columns(value, step)
        padded[j, frame, 1 : rows + 1] = moved.astype(bf16)


def clear_edges(padded):
    rows = padded.shape[2]
    zero = jnp.zeros(padded.shape[:2] + padded.shape[3:], bf16)
    padded[:, :, 0] = zero
    padded[:, :, rows - 1] = zero


def fill_hidden(padded, clip_ref, halo_ref, mean, inv, gain, bias, at_start):
    clear_edges(padded)
    frames = clip_ref.shape[0]
    lead = halo_ref.shape[0]
    for frame in range(frames + lead):
        if frame < lead:
            value = jnp.where(at_start, clip_ref[0].astype(f32), halo_ref[frame].astype(f32))
        else:
            value = clip_ref[frame - lead].astype(f32)
        affine = (value - mean) * inv * gain + bias
        hidden = affine * jax.nn.sigmoid(affine)
        place(padded, frame, hidden)


def tap_block(padded, frames, rows, t, i):
    width = padded.shape[-1]
    return [padded[j, t : t + frames, i : i + rows].reshape(-1, width) for j in range(KS)]


def weight_kernel(
    members, split,
    clip_ref, halo_ref, stats_a, stats_b, gain_ref, bias_ref, cot_ref,
    *rest,
):
    outs, (padded, total) = rest[:-2], rest[-2:]
    frames, rows, cols, width = clip_ref.shape
    out_width = cot_ref.shape[-1]
    at_start = lax.axis_index("ctx") == 0
    mean, inv = moments(stats_a, stats_b, members)
    fill_hidden(padded, clip_ref, halo_ref, mean, inv, gain_ref[...], bias_ref[...], at_start)
    cot_t = cot_ref[...].reshape(-1, out_width).T
    pieces = []
    for t in range(KT):
        for i in range(KS):
            pieces.append((t, i))
    begin = 0
    for at in range(0, len(pieces), 2):
        parts = []
        for t, i in pieces[at : at + 2]:
            parts += tap_block(padded, frames, rows, t, i)
        if at + 2 > len(pieces):
            parts.append(clip_ref[...].reshape(-1, width))
        taps = jnp.concatenate(parts, axis=1)
        part = lax.dot_general(cot_t, taps, (((1,), (0,)), ((), ())), preferred_element_type=f32)
        part = part.T
        stop = begin + part.shape[0]
        if split is None:
            outs[0][begin:stop, :] = part
        else:
            scatter_rows(total, part, begin, split)
        begin = stop
    if split is not None:
        own_ref, send_ref = outs
        core = lax.rem(lax.axis_index("dp"), 2)
        halves, blocks = total.shape[0], total.shape[1] // 2
        for half in range(halves):
            for k in range(blocks):
                own_ref[half, k] = total[half, 2 * k + core]
                send_ref[half, k] = total[half, 2 * k + 1 - core].astype(bf16)


def scatter_rows(total, part, begin, split):
    conv_rows, short_rows, conv_all = split
    halves = total.shape[0]
    row, stop = begin, begin + part.shape[0]
    width = total.shape[-1]
    while row < stop:
        if row < conv_all:
            block, offset = divmod(row, conv_rows)
            count = min(conv_rows - offset, stop - row, conv_all - row)
            target = offset
        else:
            block, offset = divmod(row - conv_all, short_rows)
            count = min(short_rows - offset, stop - row)
            target = conv_rows + offset
        for half in range(halves):
            total[half, block, target : target + count, :] = part[
                row - begin : row - begin + count, half * width : (half + 1) * width
            ]
        row += count


def forward_kernel(
    members,
    clip_ref, halo_ref, stats_a, stats_b, gain_ref, bias_ref, weight_ref, short_ref, after_ref,
    out_ref, padded,
):
    frames, rows, cols, width = clip_ref.shape
    at_start = lax.axis_index("ctx") == 0
    mean, inv = moments(stats_a, stats_b, members)
    fill_hidden(padded, clip_ref, halo_ref, mean, inv, gain_ref[...], bias_ref[...], at_start)
    for frame in range(frames):
        parts = []
        for t in range(KT):
            for i in range(KS):
                for j in range(KS):
                    parts.append(padded[j, frame + t, i : i + rows].reshape(-1, width))
        split = len(parts) * width
        result = jnp.dot(jnp.concatenate(parts, axis=1), weight_ref[...], preferred_element_type=f32)
        result = result + jnp.dot(
            clip_ref[frame].reshape(-1, width), short_ref[...], preferred_element_type=f32
        )
        out_ref[frame] = result.astype(bf16).reshape(rows, cols, -1)


def back_weights(weight_ref, width, taps_t):
    bands = []
    for t in taps_t:
        bands.append(
            jnp.concatenate(
                [weight_ref[(t * KS * KS + q) * width : (t * KS * KS + q + 1) * width, :] for q in range(KS * KS)],
                axis=1,
            )
        )
    return jnp.concatenate(bands, axis=0) if len(bands) > 1 else bands[0]


def fill_cot(padded, cot_ref):
    clear_edges(padded)
    for frame in range(cot_ref.shape[0]):
        place(padded, frame, cot_ref[frame].astype(f32))


def spatial_block(padded, frame, rows):
    out_width = padded.shape[-1]
    parts = []
    for i in range(KS):
        for j in range(KS):
            parts.append(padded[2 - j, frame, 2 - i : 2 - i + rows].reshape(-1, out_width))
    return jnp.concatenate(parts, axis=1)


def back_dot(block, weights):
    return lax.dot_general(block, weights, (((1,), (1,)), ((), ())), preferred_element_type=f32)


def back_own_kernel(cot_ref, weight_ref, out_ref, padded):
    frames, rows, cols, out_width = cot_ref.shape
    width = out_ref.shape[-1]
    at_start = lax.axis_index("ctx") == 0
    fill_cot(padded, cot_ref)
    late = back_weights(weight_ref, width, (2, 1))
    early = back_weights(weight_ref, width, (0,))
    for frame in range(frames):
        block = spatial_block(padded, frame, rows)
        both = back_dot(block, late)
        y2, y1 = both[:, :width], both[:, width:]
        y0 = back_dot(block, early)
        if frame == 0:
            out_ref[0] = y2 + jnp.where(at_start, y1 + y0, 0.0)
        else:
            out_ref[frame] = y2
            out_ref[frame - 1] += y1
            if frame == 1:
                out_ref[0] += jnp.where(at_start, y0, 0.0)
            else:
                out_ref[frame - 2] += y0


def back_rest_kernel(
    members,
    part_ref, cot_ref, weight_ref, clip_ref, stats_a, stats_b, gain_ref, bias_ref,
    grad_ref, sums_ref, padded,
):
    frames, rows, cols, width = clip_ref.shape
    fill_cot(padded, cot_ref)
    late = back_weights(weight_ref, width, (1, 0))
    early = back_weights(weight_ref, width, (0,))
    both = back_dot(spatial_block(padded, 0, rows), late)
    y1, y0 = both[:, :width], both[:, width:]
    last = back_dot(spatial_block(padded, 1, rows), early)
    mean, inv = moments(stats_a, stats_b, members)
    total = jnp.zeros((1, width), f32)
    cross = jnp.zeros((1, width), f32)
    for frame in range(frames):
        grad = part_ref[frame]
        if frame == frames - 2:
            grad = grad + y0
        if frame == frames - 1:
            grad = grad + (y1 + last)
        standard = (clip_ref[frame].reshape(-1, width).astype(f32) - mean) * inv
        affine = standard * gain_ref[...] + bias_ref[...]
        logistic = jax.nn.sigmoid(affine)
        grad = grad * logistic * (1.0 + affine * (1.0 - logistic)) * gain_ref[...]
        grad_ref[frame] = grad
        total = total + column_totals(grad)
        cross = cross + column_totals(grad * standard)
    sums_ref[...] = group_totals(two_rows(total, cross))


def finish_kernel(
    members,
    grad_ref, sums_a, sums_b, clip_ref, stats_a, stats_b, cot_ref, short_ref,
    out_ref,
):
    frames, rows, cols, width = clip_ref.shape
    out_width = cot_ref.shape[-1]
    mean, inv = moments(stats_a, stats_b, members)
    sums = sums_a[...] + sums_b[...]
    mean_grad = sums[0:1] / members
    mean_cross = sums[1:2] / members
    for frame in range(frames):
        standard = (clip_ref[frame].reshape(-1, width).astype(f32) - mean) * inv
        shortcut = back_dot(cot_ref[frame].reshape(-1, out_width), short_ref[...])
        grad = (grad_ref[frame] - mean_grad - standard * mean_cross) * inv + shortcut
        out_ref[frame] = grad.astype(bf16).reshape(rows, cols, width)


def plane_kernel(own_ref, got_ref, keep_ref, x_ref, y_ref, xy_ref):
    halves, deep, wide = own_ref.shape[:3]
    x = lax.rem(lax.axis_index("dp") // 2, 2)
    y = lax.axis_index("ctx")
    for z in range(deep):
        for half, col, target in ((y, x, keep_ref), (y, 1 - x, x_ref), (1 - y, x, y_ref), (1 - y, 1 - x, xy_ref)):
            value = own_ref[half, z, col] + got_ref[half, z, col].astype(f32)
            target[z] = value.astype(target.dtype)


def line_kernel(keep_ref, x_ref, y_ref, xy_ref, own_ref, a_ref, b_ref, c_ref):
    z = lax.axis_index("dp") // 4
    for step, target in enumerate((own_ref, a_ref, b_ref, c_ref)):
        at = lax.bitwise_xor(z, step)
        value = keep_ref[at] + x_ref[at].astype(f32) + (y_ref[at].astype(f32) + xy_ref[at].astype(f32))
        target[...] = value.astype(target.dtype)


def last_kernel(scale, own_ref, a_ref, b_ref, c_ref, conv_ref, short_ref):
    value = own_ref[...] + a_ref[...].astype(f32) + (b_ref[...].astype(f32) + c_ref[...].astype(f32))
    value = value * scale
    conv_ref[...] = value[: conv_ref.shape[0]]
    short_ref[...] = value[conv_ref.shape[0] :]


def from_behind(value, axis, steps):
    count = lax.axis_size(axis)
    initial, last = (max(0, -steps), min(count, count - steps))
    return lax.ppermute(value, axis, [(source, source + steps) for source in range(initial, last)])


def others_total(value):
    count = lax.axis_size("ctx")
    total = None
    for step in range(1, count):
        got = lax.ppermute(value, "ctx", [(source, (source + step) % count) for source in range(count)])
        total = got if total is None else total + got
    return jnp.zeros_like(value) if total is None else total


def swap(value, dp_mask, ctx_mask=0):
    dp, ctx = lax.axis_size("dp"), lax.axis_size("ctx")
    pairs = []
    for source in range(dp * ctx):
        at, side = divmod(source, ctx)
        pairs.append((source, (at ^ dp_mask) * ctx + (side ^ ctx_mask)))
    return lax.ppermute(value, ("dp", "ctx"), pairs)


def reduce_staged(own, send, conv_rows, short_rows, scale):
    halves, blocks, rows, cols = own.shape
    got = swap(send, 1)
    shape = (halves, blocks // 2, 2, rows, cols)
    part = (blocks // 2, rows, cols)
    keep, to_x, to_y, to_xy = call(
        plane_kernel,
        [jax.ShapeDtypeStruct(part, f32)] + [jax.ShapeDtypeStruct(part, bf16)] * 3,
        moved=own.size * 8,
    )(own.reshape(shape), got.reshape(shape))
    from_x, from_y, from_xy = swap(to_x, 2), swap(to_y, 0, 1), swap(to_xy, 2, 1)
    mine, to_a, to_b, to_c = call(
        line_kernel,
        [jax.ShapeDtypeStruct(part[1:], f32)] + [jax.ShapeDtypeStruct(part[1:], bf16)] * 3,
        moved=keep.size * 12,
    )(keep, from_x, from_y, from_xy)
    from_a, from_b, from_c = swap(to_a, 4), swap(to_b, 8), swap(to_c, 12)
    return call(
        functools.partial(last_kernel, scale),
        [jax.ShapeDtypeStruct((conv_rows, cols), f32), jax.ShapeDtypeStruct((short_rows, cols), f32)],
        moved=mine.size * 12,
    )(mine, from_a, from_b, from_c)


def body(clip_in, norm_gain, norm_bias, conv_weight, short_weight, out_cotangent):
    batch_clips, frames, height, breadth, in_width = clip_in.shape
    assert batch_clips == 1
    out_width = conv_weight.shape[1]
    per_group = in_width // GROUPS
    dp_size, ctx_size = lax.axis_size("dp"), lax.axis_size("ctx")
    total_frames = frames * ctx_size
    members = total_frames * height * breadth * per_group
    scale = 1.0 / (batch_clips * dp_size * total_frames)
    places = frames * height * breadth
    clip = clip_in[0]
    cot = out_cotangent[0]
    gain = norm_gain.reshape(1, in_width)
    bias = norm_bias.reshape(1, in_width)
    conv_all = TAPS * in_width
    work = places * conv_all * out_width * 2

    halo = from_behind(clip[frames - 2 :], "ctx", 1)
    following = from_behind(cot[:2], "ctx", -1)
    stats = call(stats_kernel, jax.ShapeDtypeStruct((8, in_width), f32), moved=clip.size * 2)(clip)
    other = others_total(stats)

    back_part = call(
        back_own_kernel,
        jax.ShapeDtypeStruct((frames, height * breadth, in_width), f32),
        [pltpu.VMEM((KS, frames, height + 2, breadth, out_width), bf16)],
        flops=2 * work, moved=conv_weight.size * 2,
    )(cot, conv_weight)

    padded = pltpu.VMEM((KS, frames + 2, height + 2, breadth, in_width), bf16)
    staged = dp_size == 16 and ctx_size == 2
    conv_rows, short_rows = conv_all // dp_size, in_width // dp_size
    if staged:
        cols = out_width // ctx_size
        blocks = (ctx_size, dp_size // 2, conv_rows + short_rows, cols)
        outs = [jax.ShapeDtypeStruct(blocks, f32), jax.ShapeDtypeStruct(blocks, bf16)]
        total = pltpu.VMEM((ctx_size, dp_size, conv_rows + short_rows, cols), f32)
        split = (conv_rows, short_rows, conv_all)
    else:
        outs = [jax.ShapeDtypeStruct((conv_all + in_width, out_width), f32)]
        total = pltpu.VMEM((8, 128), f32)
        split = None
    parts = call(
        functools.partial(weight_kernel, members, split), outs, [padded, total], flops=work, moved=cot.size * 2
    )(clip, halo, stats, other, gain, bias, cot)
    if staged:
        conv_grad, short_grad = reduce_staged(*parts, conv_rows, short_rows, scale)
    else:
        summed = []
        for part in (parts[0][:conv_all], parts[0][conv_all:]):
            part = lax.psum_scatter(part, "dp", scatter_dimension=0, tiled=True)
            part = lax.psum_scatter(part, "ctx", scatter_dimension=1, tiled=True)
            summed.append(part * scale)
        conv_grad, short_grad = summed

    clip_out = call(
        functools.partial(forward_kernel, members),
        jax.ShapeDtypeStruct((frames, height, breadth, out_width), bf16),
        [padded],
        flops=work, moved=conv_weight.size * 2,
    )(clip, halo, stats, other, gain, bias, conv_weight, short_weight, stats)

    grad, sums = call(
        functools.partial(back_rest_kernel, members),
        [
            jax.ShapeDtypeStruct((frames, height * breadth, in_width), f32),
            jax.ShapeDtypeStruct((8, in_width), f32),
        ],
        [pltpu.VMEM((KS, 2, height + 2, breadth, out_width), bf16)],
        flops=work, moved=conv_weight.size * 2,
    )(back_part, following, conv_weight, clip, stats, other, gain, bias)
    other_sums = others_total(sums)
    clip_grad = call(
        functools.partial(finish_kernel, members),
        jax.ShapeDtypeStruct((frames, height, breadth, in_width), bf16),
        flops=work // 20, moved=cot.size * 4,
    )(grad, sums, other_sums, clip, stats, other, cot, short_weight)
    return (clip_out[None], clip_grad[None], conv_grad, short_grad)


def solution(mesh):
    return jax.shard_map(
        body,
        mesh=mesh,
        in_specs=(
            P("dp", "ctx", None, None, None),
            P(),
            P(),
            P(),
            P(),
            P("dp", "ctx", None, None, None),
        ),
        out_specs=(
            P("dp", "ctx", None, None, None),
            P("dp", "ctx", None, None, None),
            P("dp", "ctx"),
            P("dp", "ctx"),
        ),
        check_vma=False,
    )
```

```python
import functools

import jax
import jax.numpy as jnp
from jax import lax
from jax.experimental import pallas as pl
from jax.experimental.pallas import tpu as pltpu
from jax.sharding import PartitionSpec as P

GROUPS = 32
KT = 3
KS = 3
TAPS = KT * KS * KS
VMEM_BYTES = 28 * 1024 * 1024

epsilon = 1e-06
f32 = jnp.float32
bf16 = jnp.bfloat16


def call(kernel, outs, scratch=(), flops=0, moved=0, in_specs=None):
    specs = {} if in_specs is None else {"in_specs": in_specs}
    return pl.pallas_call(
        kernel,
        out_shape=outs,
        **specs,
        scratch_shapes=list(scratch),
        compiler_params=pltpu.CompilerParams(vmem_limit_bytes=VMEM_BYTES),
        cost_estimate=pl.CostEstimate(flops=flops, bytes_accessed=moved, transcendentals=0),
    )


def group_totals(rows):
    width = rows.shape[1]
    per_group = width // GROUPS
    row = lax.broadcasted_iota(jnp.int32, (width, width), 0) // per_group
    col = lax.broadcasted_iota(jnp.int32, (width, width), 1) // per_group
    same = (row == col).astype(f32)
    return lax.dot_general(
        rows, same, (((1,), (0,)), ((), ())), precision=lax.Precision.HIGHEST, preferred_element_type=f32
    )


def two_rows(first, second):
    at = lax.broadcasted_iota(jnp.int32, (8, first.shape[1]), 0)
    return jnp.where(at == 0, first, jnp.where(at == 1, second, 0.0))


def column_totals(value):
    return jnp.sum(value, axis=0, keepdims=True)


def in_pieces(value):
    high = value.astype(bf16)
    rest = value - high.astype(f32)
    middle = rest.astype(bf16)
    low = (rest - middle.astype(f32)).astype(bf16)
    return high, middle, low


def pieces_block(totals):
    pieces = [piece[0:2].astype(f32) for piece in in_pieces(totals)]
    zero = jnp.zeros((10, totals.shape[1]), f32)
    return jnp.concatenate(pieces + [zero], axis=0).astype(bf16)


def start_kernel(clip_ref, stats_ref, parcel_ref):
    frames, rows, cols, width = clip_ref.shape
    places = rows * cols
    total = jnp.zeros((1, width), f32)
    square = jnp.zeros((1, width), f32)
    for frame in range(frames):
        value = clip_ref[frame].reshape(-1, width).astype(f32)
        total = total + column_totals(value)
        square = square + column_totals(value * value)
    totals = group_totals(two_rows(total, square))
    stats_ref[...] = totals
    lead = KT - 1
    for frame in range(lead):
        parcel_ref[frame * places : (frame + 1) * places] = clip_ref[frames - lead + frame].reshape(places, width)
    parcel_ref[lead * places :] = pieces_block(totals)


def moments(stats, parcel, members):
    pieces = parcel[parcel.shape[0] - 16 :].astype(f32)
    totals = stats[0:2] + (pieces[0:2] + (pieces[2:4] + pieces[4:6]))
    mean = totals[0:1] / members
    variance = totals[1:2] / members - mean * mean
    return mean, lax.rsqrt(variance + epsilon)


def shift_columns(value, step):
    rows, cols, width = value.shape
    flat = value.reshape(rows * cols, width)
    rolled = pltpu.roll(flat, (-step) % (rows * cols), 0).reshape(rows, cols, width)
    at = lax.broadcasted_iota(jnp.int32, (rows, cols, width), 1)
    edge = cols - 1 if step == 1 else 0
    return jnp.where(at == edge, 0.0, rolled)


def place(padded, frame, value):
    rows, cols, width = value.shape
    for j, step in enumerate((-1, 0, 1)):
        moved = value if step == 0 else shift_columns(value, step)
        padded[j, frame, 1 : rows + 1] = moved.astype(bf16)


def clear_edges(padded):
    rows = padded.shape[2]
    zero = jnp.zeros(padded.shape[:2] + padded.shape[3:], bf16)
    padded[:, :, 0] = zero
    padded[:, :, rows - 1] = zero


def hidden_of(value, mean, inv, gain, bias):
    affine = (value.astype(f32) - mean) * inv * gain + bias
    return affine * jax.nn.sigmoid(affine)


def fill_hidden(padded, clip_ref, parcel_ref, mean, inv, gain, bias):
    clear_edges(padded)
    frames, rows, cols, width = clip_ref.shape
    places = rows * cols
    lead = KT - 1
    at_start = lax.axis_index("ctx") == 0
    for frame in range(frames + lead):
        if frame < lead:
            before = parcel_ref[frame * places : (frame + 1) * places].reshape(rows, cols, width)
            value = jnp.where(at_start, clip_ref[0].astype(f32), before.astype(f32))
        else:
            value = clip_ref[frame - lead].astype(f32)
        place(padded, frame, hidden_of(value, mean, inv, gain, bias))


def tap_block(padded, frames, rows, t, i):
    width = padded.shape[-1]
    return [padded[j, t : t + frames, i : i + rows].reshape(-1, width) for j in range(KS)]


def weight_kernel(
    members, split,
    clip_ref, parcel_ref, stats_ref, gain_ref, bias_ref, cot_ref,
    padded, *rest,
):
    frames, rows, cols, width = clip_ref.shape
    out_width = cot_ref.shape[-1]
    mean, inv = moments(stats_ref, parcel_ref, members)
    fill_hidden(padded, clip_ref, parcel_ref, mean, inv, gain_ref[...], bias_ref[...])
    cot_t = cot_ref[...].reshape(-1, out_width).T
    pieces = [(t, i) for t in range(KT) for i in range(KS)]
    begin = 0
    total = rest[-1]
    for at in range(0, len(pieces), 2):
        parts = []
        for t, i in pieces[at : at + 2]:
            parts += tap_block(padded, frames, rows, t, i)
        if at + 2 > len(pieces):
            parts.append(clip_ref[...].reshape(-1, width))
        part = jnp.dot(cot_t, jnp.concatenate(parts, axis=1), preferred_element_type=f32).T
        if split is None:
            rest[0][begin : begin + part.shape[0], :] = part
        else:
            scatter_rows(total, part, begin, split)
        begin += part.shape[0]
    if split is not None:
        own_ref, send_ref = rest[:-1]
        core = lax.rem(lax.axis_index("dp"), 2)
        halves, blocks = total.shape[0], total.shape[1] // 2
        for half in range(halves):
            for k in range(blocks):
                own_ref[half, k] = total[half, 2 * k + core]
                send_ref[half, k] = total[half, 2 * k + 1 - core].astype(bf16)


def scatter_rows(total, part, begin, split):
    conv_rows, short_rows, conv_all = split
    halves = total.shape[0]
    row, stop = begin, begin + part.shape[0]
    width = total.shape[-1]
    while row < stop:
        if row < conv_all:
            block, offset = divmod(row, conv_rows)
            count = min(conv_rows - offset, stop - row, conv_all - row)
            target = offset
        else:
            block, offset = divmod(row - conv_all, short_rows)
            count = min(short_rows - offset, stop - row)
            target = conv_rows + offset
        for half in range(halves):
            total[half, block, target : target + count, :] = part[
                row - begin : row - begin + count, half * width : (half + 1) * width
            ]
        row += count


def forward_kernel(padded, clip_ref, weight_ref, short_ref, out_ref):
    frames, rows, cols, width = clip_ref.shape
    for frame in range(frames):
        parts = []
        for t in range(KT):
            for i in range(KS):
                for j in range(KS):
                    parts.append(padded[j, frame + t, i : i + rows].reshape(-1, width))
        result = jnp.dot(jnp.concatenate(parts, axis=1), weight_ref[...], preferred_element_type=f32)
        result = result + jnp.dot(
            clip_ref[frame].reshape(-1, width), short_ref[...], preferred_element_type=f32
        )
        out_ref[frame] = result.astype(bf16).reshape(rows, cols, -1)


def back_weights(weight_ref, width, taps_t):
    bands = []
    for t in taps_t:
        bands.append(
            jnp.concatenate(
                [weight_ref[(t * KS * KS + q) * width : (t * KS * KS + q + 1) * width, :] for q in range(KS * KS)],
                axis=1,
            )
        )
    return jnp.concatenate(bands, axis=0) if len(bands) > 1 else bands[0]


def fill_cot(padded, cot_ref):
    clear_edges(padded)
    for frame in range(cot_ref.shape[0]):
        place(padded, frame, cot_ref[frame].astype(f32))


def spatial_block(padded, frame, rows):
    out_width = padded.shape[-1]
    parts = []
    for i in range(KS):
        for j in range(KS):
            parts.append(padded[2 - j, frame, 2 - i : 2 - i + rows].reshape(-1, out_width))
    return jnp.concatenate(parts, axis=1)


def back_dot(block, weights):
    return lax.dot_general(block, weights, (((1,), (1,)), ((), ())), preferred_element_type=f32)


def back_kernel(cot_ref, weight_ref, out_ref, before_ref, padded):
    frames, rows, cols, out_width = cot_ref.shape
    width = out_ref.shape[-1]
    at_start = lax.axis_index("ctx") == 0
    fill_cot(padded, cot_ref)
    late = back_weights(weight_ref, width, (2, 1))
    early = back_weights(weight_ref, width, (0,))
    for frame in range(frames):
        block = spatial_block(padded, frame, rows)
        both = back_dot(block, late)
        y2, y1 = both[:, :width], both[:, width:]
        y0 = back_dot(block, early)
        if frame == 0:
            lead, next_lead = y0, y1
            out_ref[0] = y2
        else:
            out_ref[frame] = y2
            out_ref[frame - 1] += y1
            if frame == 1:
                next_lead = next_lead + y0
                before_ref[0] = lead.astype(bf16)
                before_ref[1] = next_lead.astype(bf16)
                out_ref[0] += jnp.where(at_start, lead + next_lead, 0.0)
            else:
                out_ref[frame - 2] += y0


def activation_kernel(
    members,
    part_ref, after_ref, clip_ref, parcel_ref, stats_ref, gain_ref, bias_ref,
    grad_ref, sums_ref,
):
    frames, rows, cols, width = clip_ref.shape
    mean, inv = moments(stats_ref, parcel_ref, members)
    total = jnp.zeros((1, width), f32)
    cross = jnp.zeros((1, width), f32)
    ahead = after_ref.shape[0]
    for frame in range(frames):
        grad = part_ref[frame]
        if frame >= frames - ahead:
            grad = grad + after_ref[frame - (frames - ahead)].astype(f32)
        standard = (clip_ref[frame].reshape(-1, width).astype(f32) - mean) * inv
        affine = standard * gain_ref[...] + bias_ref[...]
        logistic = jax.nn.sigmoid(affine)
        grad = grad * logistic * (1.0 + affine * (1.0 - logistic)) * gain_ref[...]
        grad_ref[frame] = grad
        total = total + column_totals(grad)
        cross = cross + column_totals(grad * standard)
    sums_ref[...] = group_totals(two_rows(total, cross))


def finish_kernel(
    members,
    grad_ref, sums_a, sums_b, clip_ref, parcel_ref, stats_ref, cot_ref, short_ref,
    out_ref,
):
    frames, rows, cols, width = clip_ref.shape
    out_width = cot_ref.shape[-1]
    mean, inv = moments(stats_ref, parcel_ref, members)
    sums = sums_a[...] + sums_b[...]
    mean_grad = sums[0:1] / members
    mean_cross = sums[1:2] / members
    for frame in range(frames):
        standard = (clip_ref[frame].reshape(-1, width).astype(f32) - mean) * inv
        shortcut = back_dot(cot_ref[frame].reshape(-1, out_width), short_ref[...])
        grad = (grad_ref[frame] - mean_grad - standard * mean_cross) * inv + shortcut
        out_ref[frame] = grad.astype(bf16).reshape(rows, cols, width)


def plane_kernel(own_ref, got_ref, keep_ref, x_ref, y_ref, xy_ref):
    halves, deep, wide = own_ref.shape[:3]
    x = lax.rem(lax.axis_index("dp") // 2, 2)
    y = lax.axis_index("ctx")
    for z in range(deep):
        for half, col, target in ((y, x, keep_ref), (y, 1 - x, x_ref), (1 - y, x, y_ref), (1 - y, 1 - x, xy_ref)):
            value = own_ref[half, z, col] + got_ref[half, z, col].astype(f32)
            target[z] = value.astype(target.dtype)


def line_kernel(keep_ref, xy_ref, x_ref, y_ref, own_ref, a_ref, b_ref, c_ref):
    z = lax.axis_index("dp") // 4
    for step, target in enumerate((own_ref, a_ref, b_ref, c_ref)):
        at = lax.bitwise_xor(z, step)
        value = keep_ref[at] + x_ref[at].astype(f32) + (y_ref[at].astype(f32) + xy_ref[at].astype(f32))
        target[...] = value.astype(target.dtype)


def last_kernel(scale, own_ref, a_ref, b_ref, c_ref, conv_ref, short_ref):
    value = own_ref[...] + a_ref[...].astype(f32) + (b_ref[...].astype(f32) + c_ref[...].astype(f32))
    value = value * scale
    conv_ref[...] = value[: conv_ref.shape[0]]
    short_ref[...] = value[conv_ref.shape[0] :]


def from_behind(value, axis, steps):
    count = lax.axis_size(axis)
    initial, last = (max(0, -steps), min(count, count - steps))
    return lax.ppermute(value, axis, [(source, source + steps) for source in range(initial, last)])


def others_total(value):
    count = lax.axis_size("ctx")
    total = None
    for step in range(1, count):
        got = lax.ppermute(value, "ctx", [(source, (source + step) % count) for source in range(count)])
        total = got if total is None else total + got
    return jnp.zeros_like(value) if total is None else total


def swap(value, dp_mask, ctx_mask=0):
    dp, ctx = lax.axis_size("dp"), lax.axis_size("ctx")
    pairs = []
    for source in range(dp * ctx):
        at, side = divmod(source, ctx)
        pairs.append((source, (at ^ dp_mask) * ctx + (side ^ ctx_mask)))
    return lax.ppermute(value, ("dp", "ctx"), pairs)


def sort_plane(own, got):
    halves, blocks, rows, cols = own.shape
    shape = (halves, blocks // 2, 2, rows, cols)
    part = (blocks // 2, rows, cols)
    return call(
        plane_kernel,
        [jax.ShapeDtypeStruct(part, f32)] + [jax.ShapeDtypeStruct(part, bf16)] * 3,
        moved=own.size * 8,
    )(own.reshape(shape), got.reshape(shape))


def sort_line(keep, *planes):
    part = keep.shape[1:]
    return call(
        line_kernel,
        [jax.ShapeDtypeStruct(part, f32)] + [jax.ShapeDtypeStruct(part, bf16)] * 3,
        moved=keep.size * 12,
    )(keep, *planes)


def add_line(mine, from_a, from_b, from_c, conv_rows, short_rows, scale):
    cols = mine.shape[1]
    return call(
        functools.partial(last_kernel, scale),
        [jax.ShapeDtypeStruct((conv_rows, cols), f32), jax.ShapeDtypeStruct((short_rows, cols), f32)],
        moved=mine.size * 12,
    )(mine, from_a, from_b, from_c)


def body(clip_in, norm_gain, norm_bias, conv_weight, short_weight, out_cotangent):
    batch_clips, frames, height, breadth, in_width = clip_in.shape
    assert batch_clips == 1
    out_width = conv_weight.shape[1]
    per_group = in_width // GROUPS
    dp_size, ctx_size = lax.axis_size("dp"), lax.axis_size("ctx")
    total_frames = frames * ctx_size
    members = total_frames * height * breadth * per_group
    scale = 1.0 / (batch_clips * dp_size * total_frames)
    places = frames * height * breadth
    clip = clip_in[0]
    cot = out_cotangent[0]
    gain = norm_gain.reshape(1, in_width)
    bias = norm_bias.reshape(1, in_width)
    conv_all = TAPS * in_width
    work = places * conv_all * out_width * 2

    lead = KT - 1
    stats, parcel = call(
        start_kernel,
        [
            jax.ShapeDtypeStruct((8, in_width), f32),
            jax.ShapeDtypeStruct((lead * height * breadth + 16, in_width), bf16),
        ],
        flops=work, moved=clip.size * 2,
    )(clip)
    if ctx_size == 2:
        before = lax.ppermute(parcel, "ctx", [(0, 1), (1, 0)])
    else:
        before = from_behind(clip[frames - lead :], "ctx", 1).reshape(-1, in_width)
        before = jnp.concatenate([before, pieces_block(others_total(stats))], axis=0)

    back_part, leading = call(
        back_kernel,
        [
            jax.ShapeDtypeStruct((frames, height * breadth, in_width), f32),
            jax.ShapeDtypeStruct((lead, height * breadth, in_width), bf16),
        ],
        [pltpu.VMEM((KS, frames, height + 2, breadth, out_width), bf16)],
        flops=2 * work, moved=conv_weight.size * 2,
    )(cot, conv_weight)
    before, back_part = lax.optimization_barrier((before, back_part))
    after = from_behind(leading, "ctx", -1)

    staged = dp_size == 16 and ctx_size == 2
    conv_rows, short_rows = conv_all // dp_size, in_width // dp_size
    if staged:
        cols = out_width // ctx_size
        blocks = (ctx_size, dp_size // 2, conv_rows + short_rows, cols)
        outs = [jax.ShapeDtypeStruct(blocks, f32), jax.ShapeDtypeStruct(blocks, bf16)]
        scratch = [pltpu.VMEM((ctx_size, dp_size, conv_rows + short_rows, cols), f32)]
        split = (conv_rows, short_rows, conv_all)
    else:
        outs = [jax.ShapeDtypeStruct((conv_all + in_width, out_width), f32)]
        scratch = []
        split = None
    hidden, *parts = call(
        functools.partial(weight_kernel, members, split),
        [jax.ShapeDtypeStruct((KS, frames + KT - 1, height + 2, breadth, in_width), bf16)] + outs,
        scratch,
        flops=work, moved=cot.size * 2,
    )(clip, before, stats, gain, bias, cot)

    after, *parts = lax.optimization_barrier((after, *parts))
    grad, sums = call(
        functools.partial(activation_kernel, members),
        [
            jax.ShapeDtypeStruct((frames, height * breadth, in_width), f32),
            jax.ShapeDtypeStruct((8, in_width), f32),
        ],
        flops=work, moved=conv_weight.size * 2,
    )(back_part, after, clip, before, stats, gain, bias)
    if staged:
        own, got, sums = lax.optimization_barrier((parts[0], swap(parts[1], 1), sums))
        keep, to_x, to_y, to_xy = sort_plane(own, got)
        from_xy, from_x, from_y = swap(to_xy, 2, 1), swap(to_x, 2), swap(to_y, 0, 1)
        planes = (from_xy, from_x, from_y)
        hidden, keep = lax.optimization_barrier((hidden, keep))
    other_sums = others_total(sums)
    clip_out = call(
        forward_kernel,
        jax.ShapeDtypeStruct((frames, height, breadth, out_width), bf16),
        flops=work, moved=conv_weight.size * 2,
    )(hidden, clip, conv_weight, short_weight)
    if staged:
        *planes, clip_out, other_sums = lax.optimization_barrier((*planes, clip_out, other_sums))
        mine, *lines = sort_line(keep, *planes)
        lines = (swap(lines[2], 12), swap(lines[1], 8), swap(lines[0], 4))
        conv_grad, short_grad = add_line(mine, *lines, conv_rows, short_rows, scale)
        grad, mine = lax.optimization_barrier((grad, mine))
    else:
        summed = []
        for part in (parts[0][:conv_all], parts[0][conv_all:]):
            part = lax.psum_scatter(part, "dp", scatter_dimension=0, tiled=True)
            part = lax.psum_scatter(part, "ctx", scatter_dimension=1, tiled=True)
            summed.append(part * scale)
        conv_grad, short_grad = summed

    clip_grad = call(
        functools.partial(finish_kernel, members),
        jax.ShapeDtypeStruct((frames, height, breadth, in_width), bf16),
        flops=work // 20, moved=cot.size * 4,
    )(grad, sums, other_sums, clip, before, stats, cot, short_weight)
    return (clip_out[None], clip_grad[None], conv_grad, short_grad)


def solution(mesh):
    return jax.shard_map(
        body,
        mesh=mesh,
        in_specs=(
            P("dp", "ctx", None, None, None),
            P(),
            P(),
            P(),
            P(),
            P("dp", "ctx", None, None, None),
        ),
        out_specs=(
            P("dp", "ctx", None, None, None),
            P("dp", "ctx", None, None, None),
            P("dp", "ctx"),
            P("dp", "ctx"),
        ),
        check_vma=False,
    )
```

```python
import functools

import jax
import jax.numpy as jnp
from jax import lax
from jax.experimental import pallas as pl
from jax.experimental.pallas import tpu as pltpu
from jax.sharding import PartitionSpec as P

GROUPS = 32
KT = 3
KS = 3
TAPS = KT * KS * KS
VMEM_BYTES = 28 * 1024 * 1024

epsilon = 1e-06
f32 = jnp.float32
bf16 = jnp.bfloat16


def call(kernel, outs, scratch=(), flops=0, moved=0, in_specs=None):
    specs = {} if in_specs is None else {"in_specs": in_specs}
    return pl.pallas_call(
        kernel,
        out_shape=outs,
        **specs,
        scratch_shapes=list(scratch),
        compiler_params=pltpu.CompilerParams(vmem_limit_bytes=VMEM_BYTES),
        cost_estimate=pl.CostEstimate(flops=flops, bytes_accessed=moved, transcendentals=0),
    )


def group_totals(rows):
    width = rows.shape[1]
    per_group = width // GROUPS
    row = lax.broadcasted_iota(jnp.int32, (width, width), 0) // per_group
    col = lax.broadcasted_iota(jnp.int32, (width, width), 1) // per_group
    same = (row == col).astype(f32)
    return lax.dot_general(
        rows, same, (((1,), (0,)), ((), ())), precision=lax.Precision.HIGHEST, preferred_element_type=f32
    )


def two_rows(first, second):
    at = lax.broadcasted_iota(jnp.int32, (8, first.shape[1]), 0)
    return jnp.where(at == 0, first, jnp.where(at == 1, second, 0.0))


def column_totals(value):
    return jnp.sum(value, axis=0, keepdims=True)


def in_pieces(value):
    high = value.astype(bf16)
    rest = value - high.astype(f32)
    middle = rest.astype(bf16)
    low = (rest - middle.astype(f32)).astype(bf16)
    return high, middle, low


def pieces_block(totals):
    pieces = [piece[0:2].astype(f32) for piece in in_pieces(totals)]
    zero = jnp.zeros((10, totals.shape[1]), f32)
    return jnp.concatenate(pieces + [zero], axis=0).astype(bf16)


def start_kernel(clip_ref, stats_ref, parcel_ref):
    frames, rows, cols, width = clip_ref.shape
    places = rows * cols
    total = jnp.zeros((1, width), f32)
    square = jnp.zeros((1, width), f32)
    for frame in range(frames):
        value = clip_ref[frame].reshape(-1, width).astype(f32)
        total = total + column_totals(value)
        square = square + column_totals(value * value)
    totals = group_totals(two_rows(total, square))
    stats_ref[...] = totals
    lead = KT - 1
    for frame in range(lead):
        parcel_ref[frame * places : (frame + 1) * places] = clip_ref[frames - lead + frame].reshape(places, width)
    parcel_ref[lead * places :] = pieces_block(totals)


def whole(parcel):
    pieces = parcel[parcel.shape[0] - 16 :].astype(f32)
    return pieces[0:2] + (pieces[2:4] + pieces[4:6])


def moments(stats, parcel, members):
    totals = stats[0:2] + whole(parcel)
    mean = totals[0:1] / members
    variance = totals[1:2] / members - mean * mean
    return mean, lax.rsqrt(variance + epsilon)


def shift_columns(value, step):
    rows, cols, width = value.shape
    flat = value.reshape(rows * cols, width)
    rolled = pltpu.roll(flat, (-step) % (rows * cols), 0).reshape(rows, cols, width)
    at = lax.broadcasted_iota(jnp.int32, (rows, cols, width), 1)
    edge = cols - 1 if step == 1 else 0
    return jnp.where(at == edge, 0.0, rolled)


def place(padded, frame, value):
    rows, cols, width = value.shape
    for j, step in enumerate((-1, 0, 1)):
        moved = value if step == 0 else shift_columns(value, step)
        padded[j, frame, 1 : rows + 1] = moved.astype(bf16)


def clear_edges(padded):
    rows = padded.shape[2]
    zero = jnp.zeros(padded.shape[:2] + padded.shape[3:], bf16)
    padded[:, :, 0] = zero
    padded[:, :, rows - 1] = zero


def hidden_of(value, mean, inv, gain, bias):
    affine = (value.astype(f32) - mean) * inv * gain + bias
    return affine * jax.nn.sigmoid(affine)


def fill_hidden(padded, clip_ref, parcel_ref, mean, inv, gain, bias):
    clear_edges(padded)
    frames, rows, cols, width = clip_ref.shape
    places = rows * cols
    lead = KT - 1
    at_start = lax.axis_index("ctx") == 0
    for frame in range(frames + lead):
        if frame < lead:
            before = parcel_ref[frame * places : (frame + 1) * places].reshape(rows, cols, width)
            value = jnp.where(at_start, clip_ref[0].astype(f32), before.astype(f32))
        else:
            value = clip_ref[frame - lead].astype(f32)
        place(padded, frame, hidden_of(value, mean, inv, gain, bias))


def tap_block(padded, frames, rows, t, i):
    width = padded.shape[-1]
    return [padded[j, t : t + frames, i : i + rows].reshape(-1, width) for j in range(KS)]


def weight_kernel(
    members, split,
    clip_ref, parcel_ref, stats_ref, gain_ref, bias_ref, cot_t_ref,
    padded, total, *rest,
):
    frames, rows, cols, width = clip_ref.shape
    mean, inv = moments(stats_ref, parcel_ref, members)
    fill_hidden(padded, clip_ref, parcel_ref, mean, inv, gain_ref[...], bias_ref[...])
    cot_t = cot_t_ref[...]
    pieces = [(t, i) for t in range(KT) for i in range(KS)]
    begin = 0
    for at in range(0, len(pieces), 2):
        parts = []
        for t, i in pieces[at : at + 2]:
            parts += tap_block(padded, frames, rows, t, i)
        if at + 2 > len(pieces):
            parts.append(clip_ref[...].reshape(-1, width))
        part = jnp.dot(cot_t, jnp.concatenate(parts, axis=1), preferred_element_type=f32).T
        if split is None:
            total[begin : begin + part.shape[0], :] = part
        else:
            scatter_rows(total, part, begin, split)
        begin += part.shape[0]
    if split is not None:
        (send_ref,) = rest
        core = lax.rem(lax.axis_index("dp"), 2)
        halves, blocks = send_ref.shape[:2]
        for half in range(halves):
            for k in range(blocks):
                send_ref[half, k] = total[half, 2 * k + 1 - core].astype(bf16)


def scatter_rows(total, part, begin, split):
    conv_rows, short_rows, conv_all = split
    halves = total.shape[0]
    row, stop = begin, begin + part.shape[0]
    width = total.shape[-1]
    while row < stop:
        if row < conv_all:
            block, offset = divmod(row, conv_rows)
            count = min(conv_rows - offset, stop - row, conv_all - row)
            target = offset
        else:
            block, offset = divmod(row - conv_all, short_rows)
            count = min(short_rows - offset, stop - row)
            target = conv_rows + offset
        for half in range(halves):
            total[half, block, target : target + count, :] = part[
                row - begin : row - begin + count, half * width : (half + 1) * width
            ]
        row += count


def forward_kernel(padded, clip_ref, weight_ref, short_ref, out_ref):
    frames, rows, cols, width = clip_ref.shape
    for frame in range(frames):
        parts = []
        for t in range(KT):
            for i in range(KS):
                for j in range(KS):
                    parts.append(padded[j, frame + t, i : i + rows].reshape(-1, width))
        result = jnp.dot(jnp.concatenate(parts, axis=1), weight_ref[...], preferred_element_type=f32)
        result = result + jnp.dot(
            clip_ref[frame].reshape(-1, width), short_ref[...], preferred_element_type=f32
        )
        out_ref[frame] = result.astype(bf16).reshape(rows, cols, -1)


def back_weights(weight_ref, width, taps_t):
    bands = []
    for t in taps_t:
        bands.append(
            jnp.concatenate(
                [weight_ref[(t * KS * KS + q) * width : (t * KS * KS + q + 1) * width, :] for q in range(KS * KS)],
                axis=1,
            )
        )
    return jnp.concatenate(bands, axis=0) if len(bands) > 1 else bands[0]


def fill_cot(padded, cot_ref):
    clear_edges(padded)
    for frame in range(cot_ref.shape[0]):
        place(padded, frame, cot_ref[frame].astype(f32))


def spatial_block(padded, frame, rows):
    out_width = padded.shape[-1]
    parts = []
    for i in range(KS):
        for j in range(KS):
            parts.append(padded[2 - j, frame, 2 - i : 2 - i + rows].reshape(-1, out_width))
    return jnp.concatenate(parts, axis=1)


def back_dot(block, weights):
    return lax.dot_general(block, weights, (((1,), (1,)), ((), ())), preferred_element_type=f32)


def back_kernel(cot_ref, weight_ref, out_ref, before_ref, cot_t_ref, padded):
    frames, rows, cols, out_width = cot_ref.shape
    width = out_ref.shape[-1]
    at_start = lax.axis_index("ctx") == 0
    cot_t_ref[...] = cot_ref[...].reshape(-1, out_width).T
    fill_cot(padded, cot_ref)
    late = back_weights(weight_ref, width, (2, 1))
    early = back_weights(weight_ref, width, (0,))
    for frame in range(frames):
        block = spatial_block(padded, frame, rows)
        both = back_dot(block, late)
        y2, y1 = both[:, :width], both[:, width:]
        y0 = back_dot(block, early)
        if frame == 0:
            lead, next_lead = y0, y1
            out_ref[0] = y2
        else:
            out_ref[frame] = y2
            out_ref[frame - 1] += y1
            if frame == 1:
                next_lead = next_lead + y0
                before_ref[0] = lead.astype(bf16)
                before_ref[1] = next_lead.astype(bf16)
                out_ref[0] += jnp.where(at_start, lead + next_lead, 0.0)
            else:
                out_ref[frame - 2] += y0


def activation_kernel(
    members,
    part_ref, leading_ref, clip_ref, parcel_ref, stats_ref, gain_ref, bias_ref,
    grad_ref, slope_ref, sums_ref, out_ref,
):
    frames, rows, cols, width = clip_ref.shape
    places = rows * cols
    gain = gain_ref[...]
    mean, inv = moments(stats_ref, parcel_ref, members)

    def standard_and_slope(value):
        standard = (value.astype(f32) - mean) * inv
        affine = standard * gain + bias_ref[...]
        logistic = jax.nn.sigmoid(affine)
        return standard, logistic * (1.0 + affine * (1.0 - logistic)) * gain

    total = jnp.zeros((1, width), f32)
    cross = jnp.zeros((1, width), f32)
    lead = leading_ref.shape[0]
    for frame in range(lead):
        here = slice(frame * places, (frame + 1) * places)
        standard, slope = standard_and_slope(parcel_ref[here])
        grad = leading_ref[frame].astype(f32) * slope
        total = total + column_totals(grad)
        cross = cross + column_totals(grad * standard)
        out_ref[here] = leading_ref[frame]
    at_start = lax.axis_index("ctx") == 0
    total = jnp.where(at_start, 0.0, total)
    cross = jnp.where(at_start, 0.0, cross)
    for frame in range(frames):
        standard, slope = standard_and_slope(clip_ref[frame].reshape(-1, width))
        grad = part_ref[frame] * slope
        grad_ref[frame] = grad
        if frame >= frames - lead:
            slope_ref[frame - (frames - lead)] = slope
        total = total + column_totals(grad)
        cross = cross + column_totals(grad * standard)
    sums = group_totals(two_rows(total, cross))
    sums_ref[...] = sums
    out_ref[lead * places :] = pieces_block(sums)


def finish_kernel(
    members,
    grad_ref, slope_ref, sums_ref, after_ref, clip_ref, parcel_ref, stats_ref, cot_ref, short_ref,
    out_ref,
):
    frames, rows, cols, width = clip_ref.shape
    places = rows * cols
    out_width = cot_ref.shape[-1]
    lead = slope_ref.shape[0]
    is_last = lax.axis_index("ctx") == lax.axis_size("ctx") - 1
    mean, inv = moments(stats_ref, parcel_ref, members)
    sums = sums_ref[0:2] + whole(after_ref)
    mean_grad = sums[0:1] / members
    mean_cross = sums[1:2] / members
    for frame in range(frames):
        standard = (clip_ref[frame].reshape(-1, width).astype(f32) - mean) * inv
        shortcut = back_dot(cot_ref[frame].reshape(-1, out_width), short_ref[...])
        grad = grad_ref[frame]
        at = frame - (frames - lead)
        if at >= 0:
            following = after_ref[at * places : (at + 1) * places].astype(f32) * slope_ref[at]
            grad = grad + jnp.where(is_last, 0.0, following)
        grad = (grad - mean_grad - standard * mean_cross) * inv + shortcut
        out_ref[frame] = grad.astype(bf16).reshape(rows, cols, width)


def plane_kernel(own_ref, got_ref, keep_ref, x_ref, y_ref, xy_ref):
    deep = got_ref.shape[1]
    core = lax.rem(lax.axis_index("dp"), 2)
    x = lax.rem(lax.axis_index("dp") // 2, 2)
    y = lax.axis_index("ctx")
    for z in range(deep):
        for half, col, target in ((y, x, keep_ref), (y, 1 - x, x_ref), (1 - y, x, y_ref), (1 - y, 1 - x, xy_ref)):
            value = own_ref[half, z, col, core] + got_ref[half, z, col].astype(f32)
            target[z] = value.astype(target.dtype)


def line_kernel(keep_ref, xy_ref, x_ref, y_ref, own_ref, a_ref, b_ref, c_ref):
    z = lax.axis_index("dp") // 4
    for step, target in enumerate((own_ref, a_ref, b_ref, c_ref)):
        at = lax.bitwise_xor(z, step)
        value = keep_ref[at] + x_ref[at].astype(f32) + (y_ref[at].astype(f32) + xy_ref[at].astype(f32))
        target[...] = value.astype(target.dtype)


def last_kernel(scale, own_ref, a_ref, b_ref, c_ref, conv_ref, short_ref):
    value = own_ref[...] + a_ref[...].astype(f32) + (b_ref[...].astype(f32) + c_ref[...].astype(f32))
    value = value * scale
    conv_ref[...] = value[: conv_ref.shape[0]]
    short_ref[...] = value[conv_ref.shape[0] :]


def from_behind(value, axis, steps):
    count = lax.axis_size(axis)
    initial, last = (max(0, -steps), min(count, count - steps))
    return lax.ppermute(value, axis, [(source, source + steps) for source in range(initial, last)])


def others_total(value):
    count = lax.axis_size("ctx")
    total = None
    for step in range(1, count):
        got = lax.ppermute(value, "ctx", [(source, (source + step) % count) for source in range(count)])
        total = got if total is None else total + got
    return jnp.zeros_like(value) if total is None else total


def swap(value, dp_mask, ctx_mask=0):
    dp, ctx = lax.axis_size("dp"), lax.axis_size("ctx")
    pairs = []
    for source in range(dp * ctx):
        at, side = divmod(source, ctx)
        pairs.append((source, (at ^ dp_mask) * ctx + (side ^ ctx_mask)))
    return lax.ppermute(value, ("dp", "ctx"), pairs)


def sort_plane(total, got):
    halves, blocks, rows, cols = got.shape
    part = (blocks // 2, rows, cols)
    return call(
        plane_kernel,
        [jax.ShapeDtypeStruct(part, f32)] + [jax.ShapeDtypeStruct(part, bf16)] * 3,
    )(total.reshape(halves, blocks // 2, 2, 2, rows, cols), got.reshape(halves, blocks // 2, 2, rows, cols))


def sort_line(keep, *planes):
    part = keep.shape[1:]
    return call(
        line_kernel,
        [jax.ShapeDtypeStruct(part, f32)] + [jax.ShapeDtypeStruct(part, bf16)] * 3,
        moved=keep.size * 12,
    )(keep, *planes)


def add_line(mine, from_a, from_b, from_c, conv_rows, short_rows, scale):
    cols = mine.shape[1]
    return call(
        functools.partial(last_kernel, scale),
        [jax.ShapeDtypeStruct((conv_rows, cols), f32), jax.ShapeDtypeStruct((short_rows, cols), f32)],
        moved=mine.size * 12,
    )(mine, from_a, from_b, from_c)


def body(clip_in, norm_gain, norm_bias, conv_weight, short_weight, out_cotangent):
    batch_clips, frames, height, breadth, in_width = clip_in.shape
    assert batch_clips == 1
    out_width = conv_weight.shape[1]
    per_group = in_width // GROUPS
    dp_size, ctx_size = lax.axis_size("dp"), lax.axis_size("ctx")
    total_frames = frames * ctx_size
    members = total_frames * height * breadth * per_group
    scale = 1.0 / (batch_clips * dp_size * total_frames)
    places = frames * height * breadth
    clip = clip_in[0]
    cot = out_cotangent[0]
    gain = norm_gain.reshape(1, in_width)
    bias = norm_bias.reshape(1, in_width)
    conv_all = TAPS * in_width
    work = places * conv_all * out_width * 2

    lead = KT - 1
    stats, parcel = call(
        start_kernel,
        [
            jax.ShapeDtypeStruct((8, in_width), f32),
            jax.ShapeDtypeStruct((lead * height * breadth + 16, in_width), bf16),
        ],
        flops=work, moved=clip.size * 2,
    )(clip)
    if ctx_size == 2:
        before = lax.ppermute(parcel, "ctx", [(0, 1), (1, 0)])
    else:
        before = from_behind(clip[frames - lead :], "ctx", 1).reshape(-1, in_width)
        before = jnp.concatenate([before, pieces_block(others_total(stats))], axis=0)

    back_part, leading, cot_t = call(
        back_kernel,
        [
            jax.ShapeDtypeStruct((frames, height * breadth, in_width), f32),
            jax.ShapeDtypeStruct((lead, height * breadth, in_width), bf16),
            jax.ShapeDtypeStruct((out_width, places), bf16),
        ],
        [pltpu.VMEM((KS, frames, height + 2, breadth, out_width), bf16)],
        flops=2 * work, moved=conv_weight.size * 2,
    )(cot, conv_weight)
    before, back_part = lax.optimization_barrier((before, back_part))

    staged = dp_size == 16 and ctx_size == 2
    conv_rows, short_rows = conv_all // dp_size, in_width // dp_size
    if staged:
        cols = out_width // ctx_size
        block = (conv_rows + short_rows, cols)
        outs = [
            jax.ShapeDtypeStruct((ctx_size, dp_size) + block, f32),
            jax.ShapeDtypeStruct((ctx_size, dp_size // 2) + block, bf16),
        ]
        split = (conv_rows, short_rows, conv_all)
    else:
        outs = [jax.ShapeDtypeStruct((conv_all + in_width, out_width), f32)]
        split = None
    hidden, *parts = call(
        functools.partial(weight_kernel, members, split),
        [jax.ShapeDtypeStruct((KS, frames + lead, height + 2, breadth, in_width), bf16)] + outs,
        flops=work, moved=cot.size * 2,
    )(clip, before, stats, gain, bias, cot_t)

    if staged:
        keep, to_x, to_y, to_xy = sort_plane(parts[0], swap(parts[1], 1))
        planes = (swap(to_xy, 2, 1), swap(to_x, 2), swap(to_y, 0, 1))
        hidden, keep = lax.optimization_barrier((hidden, keep))
    clip_out = call(
        forward_kernel,
        jax.ShapeDtypeStruct((frames, height, breadth, out_width), bf16),
        flops=work // 4,
    )(hidden, clip, conv_weight, short_weight)
    leading, clip_out = lax.optimization_barrier((leading, clip_out))
    parcel_shape = jax.ShapeDtypeStruct((lead * height * breadth + 16, in_width), bf16)
    grad, slope, sums, parcel = call(
        functools.partial(activation_kernel, members),
        [
            jax.ShapeDtypeStruct((frames, height * breadth, in_width), f32),
            jax.ShapeDtypeStruct((lead, height * breadth, in_width), f32),
            jax.ShapeDtypeStruct((8, in_width), f32),
            parcel_shape,
        ],
    )(back_part, leading, clip, before, stats, gain, bias)
    if ctx_size == 2:
        after = lax.ppermute(parcel, "ctx", [(0, 1), (1, 0)])
    else:
        after = from_behind(leading, "ctx", -1).reshape(-1, in_width)
        after = jnp.concatenate([after, pieces_block(others_total(sums))], axis=0)
    if staged:
        *planes, sums = lax.optimization_barrier((*planes, sums))
        mine, *lines = sort_line(keep, *planes)
        lines = (swap(lines[2], 12), swap(lines[1], 8), swap(lines[0], 4))
        conv_grad, short_grad = add_line(mine, *lines, conv_rows, short_rows, scale)
        after, mine = lax.optimization_barrier((after, mine))
    else:
        summed = []
        for part in (parts[0][:conv_all], parts[0][conv_all:]):
            part = lax.psum_scatter(part, "dp", scatter_dimension=0, tiled=True)
            part = lax.psum_scatter(part, "ctx", scatter_dimension=1, tiled=True)
            summed.append(part * scale)
        conv_grad, short_grad = summed
    clip_grad = call(
        functools.partial(finish_kernel, members),
        jax.ShapeDtypeStruct((frames, height, breadth, in_width), bf16),
        flops=work // 20, moved=cot.size * 4,
    )(grad, slope, sums, after, clip, before, stats, cot, short_weight)
    return (clip_out[None], clip_grad[None], conv_grad, short_grad)


def solution(mesh):
    return jax.shard_map(
        body,
        mesh=mesh,
        in_specs=(
            P("dp", "ctx", None, None, None),
            P(),
            P(),
            P(),
            P(),
            P("dp", "ctx", None, None, None),
        ),
        out_specs=(
            P("dp", "ctx", None, None, None),
            P("dp", "ctx", None, None, None),
            P("dp", "ctx"),
            P("dp", "ctx"),
        ),
        check_vma=False,
    )
```

```python
import functools

import jax
import jax.numpy as jnp
from jax import lax
from jax.experimental import pallas as pl
from jax.experimental.pallas import tpu as pltpu
from jax.sharding import PartitionSpec as P

GROUPS = 32
KT = 3
KS = 3
TAPS = KT * KS * KS
VMEM_BYTES = 28 * 1024 * 1024

epsilon = 1e-06
f32 = jnp.float32
bf16 = jnp.bfloat16


def call(kernel, outs, scratch=(), flops=0, moved=0, in_specs=None):
    specs = {} if in_specs is None else {"in_specs": in_specs}
    return pl.pallas_call(
        kernel,
        out_shape=outs,
        **specs,
        scratch_shapes=list(scratch),
        compiler_params=pltpu.CompilerParams(vmem_limit_bytes=VMEM_BYTES),
        cost_estimate=pl.CostEstimate(flops=flops, bytes_accessed=moved, transcendentals=0),
    )


def group_totals(rows):
    width = rows.shape[1]
    per_group = width // GROUPS
    row = lax.broadcasted_iota(jnp.int32, (width, width), 0) // per_group
    col = lax.broadcasted_iota(jnp.int32, (width, width), 1) // per_group
    same = (row == col).astype(f32)
    return lax.dot_general(
        rows, same, (((1,), (0,)), ((), ())), precision=lax.Precision.HIGHEST, preferred_element_type=f32
    )


def two_rows(first, second):
    at = lax.broadcasted_iota(jnp.int32, (8, first.shape[1]), 0)
    return jnp.where(at == 0, first, jnp.where(at == 1, second, 0.0))


def column_totals(value):
    return jnp.sum(value, axis=0, keepdims=True)


def in_pieces(value):
    high = value.astype(bf16)
    rest = value - high.astype(f32)
    middle = rest.astype(bf16)
    low = (rest - middle.astype(f32)).astype(bf16)
    return high, middle, low


def pieces_block(totals):
    pieces = [piece[0:2].astype(f32) for piece in in_pieces(totals)]
    zero = jnp.zeros((10, totals.shape[1]), f32)
    return jnp.concatenate(pieces + [zero], axis=0).astype(bf16)


def start_kernel(clip_ref, stats_ref, parcel_ref):
    frames, rows, cols, width = clip_ref.shape
    places = rows * cols
    total = jnp.zeros((1, width), f32)
    square = jnp.zeros((1, width), f32)
    for frame in range(frames):
        value = clip_ref[frame].reshape(-1, width).astype(f32)
        total = total + column_totals(value)
        square = square + column_totals(value * value)
    totals = group_totals(two_rows(total, square))
    stats_ref[...] = totals
    lead = KT - 1
    for frame in range(lead):
        parcel_ref[frame * places : (frame + 1) * places] = clip_ref[frames - lead + frame].reshape(places, width)
    parcel_ref[lead * places :] = pieces_block(totals)


def whole(parcel):
    pieces = parcel[parcel.shape[0] - 16 :].astype(f32)
    return pieces[0:2] + (pieces[2:4] + pieces[4:6])


def moments(stats, parcel, members):
    totals = stats[0:2] + whole(parcel)
    mean = totals[0:1] / members
    variance = totals[1:2] / members - mean * mean
    return mean, lax.rsqrt(variance + epsilon)


def shift_columns(value, step):
    rows, cols, width = value.shape
    flat = value.reshape(rows * cols, width)
    rolled = pltpu.roll(flat, (-step) % (rows * cols), 0).reshape(rows, cols, width)
    at = lax.broadcasted_iota(jnp.int32, (rows, cols, width), 1)
    edge = cols - 1 if step == 1 else 0
    return jnp.where(at == edge, 0.0, rolled)


def place(padded, frame, value):
    rows, cols, width = value.shape
    for j, step in enumerate((-1, 0, 1)):
        moved = value if step == 0 else shift_columns(value, step)
        padded[j, frame, 1 : rows + 1] = moved.astype(bf16)


def clear_edges(padded):
    rows = padded.shape[2]
    zero = jnp.zeros(padded.shape[:2] + padded.shape[3:], bf16)
    padded[:, :, 0] = zero
    padded[:, :, rows - 1] = zero


def hidden_of(value, mean, inv, gain, bias):
    affine = (value.astype(f32) - mean) * inv * gain + bias
    return affine * jax.nn.sigmoid(affine)


def fill_hidden(padded, clip_ref, parcel_ref, mean, inv, gain, bias, begin, stop):
    frames, rows, cols, width = clip_ref.shape
    places = rows * cols
    lead = KT - 1
    at_start = lax.axis_index("ctx") == 0
    for frame in range(begin, stop):
        if frame < lead:
            before = parcel_ref[frame * places : (frame + 1) * places].reshape(rows, cols, width)
            value = jnp.where(at_start, clip_ref[0].astype(f32), before.astype(f32))
        else:
            value = clip_ref[frame - lead].astype(f32)
        place(padded, frame, hidden_of(value, mean, inv, gain, bias))


def tap_block(padded, frames, rows, t, i):
    width = padded.shape[-1]
    return [padded[j, t : t + frames, i : i + rows].reshape(-1, width) for j in range(KS)]


def weight_kernel(
    members, split,
    clip_ref, parcel_ref, stats_ref, gain_ref, bias_ref, cot_t_ref,
    padded, total, *rest,
):
    frames, rows, cols, width = clip_ref.shape
    mean, inv = moments(stats_ref, parcel_ref, members)
    clear_edges(padded)
    filled = 0
    cot_t = cot_t_ref[...]
    pieces = [(t, i) for t in range(KT) for i in range(KS)]
    begin = 0
    for at in range(0, len(pieces), 2):
        parts = []
        needed = pieces[at : at + 2][-1][0] + frames
        fill_hidden(padded, clip_ref, parcel_ref, mean, inv, gain_ref[...], bias_ref[...], filled, needed)
        filled = needed
        for t, i in pieces[at : at + 2]:
            parts += tap_block(padded, frames, rows, t, i)
        if at + 2 > len(pieces):
            parts.append(clip_ref[...].reshape(-1, width))
        part = jnp.dot(cot_t, jnp.concatenate(parts, axis=1), preferred_element_type=f32).T
        if split is None:
            total[begin : begin + part.shape[0], :] = part
        else:
            scatter_rows(total, part, begin, split)
        begin += part.shape[0]
    if split is not None:
        (send_ref,) = rest
        core = lax.rem(lax.axis_index("dp"), 2)
        halves, blocks = send_ref.shape[:2]
        for half in range(halves):
            for k in range(blocks):
                send_ref[half, k] = total[half, 2 * k + 1 - core].astype(bf16)


def scatter_rows(total, part, begin, split):
    conv_rows, short_rows, conv_all = split
    halves = total.shape[0]
    row, stop = begin, begin + part.shape[0]
    width = total.shape[-1]
    while row < stop:
        if row < conv_all:
            block, offset = divmod(row, conv_rows)
            count = min(conv_rows - offset, stop - row, conv_all - row)
            target = offset
        else:
            block, offset = divmod(row - conv_all, short_rows)
            count = min(short_rows - offset, stop - row)
            target = conv_rows + offset
        for half in range(halves):
            total[half, block, target : target + count, :] = part[
                row - begin : row - begin + count, half * width : (half + 1) * width
            ]
        row += count


def forward_kernel(begin, padded, clip_ref, weight_ref, short_ref, *rest):
    out_ref = rest[-1]
    rows, cols, width = clip_ref.shape[1:]
    for at in range(out_ref.shape[0]):
        frame = begin + at
        parts = []
        for t in range(KT):
            for i in range(KS):
                for j in range(KS):
                    parts.append(padded[j, frame + t, i : i + rows].reshape(-1, width))
        result = jnp.dot(jnp.concatenate(parts, axis=1), weight_ref[...], preferred_element_type=f32)
        result = result + jnp.dot(
            clip_ref[frame].reshape(-1, width), short_ref[...], preferred_element_type=f32
        )
        out_ref[at] = result.astype(bf16).reshape(rows, cols, -1)


def forward_half(half, hidden, clip, conv_weight, short_weight, whole=None):
    frames, height, breadth, _ = clip.shape
    out_width = conv_weight.shape[1]
    count = frames // 2
    flops = 2 * conv_weight.size * count * height * breadth
    vmem = pl.BlockSpec(memory_space=pltpu.VMEM)
    operands = [hidden, clip, conv_weight, short_weight] + ([] if whole is None else [whole])
    return pl.pallas_call(
        functools.partial(forward_kernel, half * count),
        out_shape=jax.ShapeDtypeStruct((frames, height, breadth, out_width), bf16),
        grid=(1,),
        in_specs=[vmem] * 4 + ([] if whole is None else [pl.BlockSpec(memory_space=pl.ANY)]),
        out_specs=pl.BlockSpec((count, height, breadth, out_width), lambda step: (half, 0, 0, 0)),
        input_output_aliases={} if whole is None else {4: 0},
        compiler_params=pltpu.CompilerParams(vmem_limit_bytes=VMEM_BYTES),
        cost_estimate=pl.CostEstimate(flops=flops // 4, bytes_accessed=0, transcendentals=0),
    )(*operands)


def back_weights(weight_ref, width, taps_t):
    bands = []
    for t in taps_t:
        bands.append(
            jnp.concatenate(
                [weight_ref[(t * KS * KS + q) * width : (t * KS * KS + q + 1) * width, :] for q in range(KS * KS)],
                axis=1,
            )
        )
    return jnp.concatenate(bands, axis=0) if len(bands) > 1 else bands[0]


def fill_cot(padded, cot_ref):
    clear_edges(padded)
    for frame in range(cot_ref.shape[0]):
        place(padded, frame, cot_ref[frame].astype(f32))


def spatial_block(padded, frame, rows):
    out_width = padded.shape[-1]
    parts = []
    for i in range(KS):
        for j in range(KS):
            parts.append(padded[2 - j, frame, 2 - i : 2 - i + rows].reshape(-1, out_width))
    return jnp.concatenate(parts, axis=1)


def back_dot(block, weights):
    return lax.dot_general(block, weights, (((1,), (1,)), ((), ())), preferred_element_type=f32)


def back_kernel(cot_ref, weight_ref, out_ref, before_ref, cot_t_ref, padded):
    frames, rows, cols, out_width = cot_ref.shape
    width = out_ref.shape[-1]
    at_start = lax.axis_index("ctx") == 0
    cot_t_ref[...] = cot_ref[...].reshape(-1, out_width).T
    fill_cot(padded, cot_ref)
    late = back_weights(weight_ref, width, (2, 1))
    early = back_weights(weight_ref, width, (0,))
    for frame in range(frames):
        block = spatial_block(padded, frame, rows)
        both = back_dot(block, late)
        y2, y1 = both[:, :width], both[:, width:]
        y0 = back_dot(block, early)
        if frame == 0:
            lead, next_lead = y0, y1
            out_ref[0] = y2
        else:
            out_ref[frame] = y2
            out_ref[frame - 1] += y1
            if frame == 1:
                next_lead = next_lead + y0
                before_ref[0] = lead.astype(bf16)
                before_ref[1] = next_lead.astype(bf16)
                out_ref[0] += jnp.where(at_start, lead + next_lead, 0.0)
            else:
                out_ref[frame - 2] += y0


def activation_kernel(
    members,
    part_ref, leading_ref, clip_ref, parcel_ref, stats_ref, gain_ref, bias_ref,
    grad_ref, slope_ref, sums_ref, out_ref,
):
    frames, rows, cols, width = clip_ref.shape
    places = rows * cols
    gain = gain_ref[...]
    mean, inv = moments(stats_ref, parcel_ref, members)

    def standard_and_slope(value):
        standard = (value.astype(f32) - mean) * inv
        affine = standard * gain + bias_ref[...]
        logistic = jax.nn.sigmoid(affine)
        return standard, logistic * (1.0 + affine * (1.0 - logistic)) * gain

    total = jnp.zeros((1, width), f32)
    cross = jnp.zeros((1, width), f32)
    lead = leading_ref.shape[0]
    for frame in range(lead):
        here = slice(frame * places, (frame + 1) * places)
        standard, slope = standard_and_slope(parcel_ref[here])
        grad = leading_ref[frame].astype(f32) * slope
        total = total + column_totals(grad)
        cross = cross + column_totals(grad * standard)
        out_ref[here] = leading_ref[frame]
    at_start = lax.axis_index("ctx") == 0
    total = jnp.where(at_start, 0.0, total)
    cross = jnp.where(at_start, 0.0, cross)
    for frame in range(frames):
        standard, slope = standard_and_slope(clip_ref[frame].reshape(-1, width))
        grad = part_ref[frame] * slope
        grad_ref[frame] = grad
        if frame >= frames - lead:
            slope_ref[frame - (frames - lead)] = slope
        total = total + column_totals(grad)
        cross = cross + column_totals(grad * standard)
    sums = group_totals(two_rows(total, cross))
    sums_ref[...] = sums
    out_ref[lead * places :] = pieces_block(sums)


def finish_kernel(
    members,
    grad_ref, slope_ref, sums_ref, after_ref, clip_ref, parcel_ref, stats_ref, cot_ref, short_ref,
    out_ref,
):
    frames, rows, cols, width = clip_ref.shape
    places = rows * cols
    out_width = cot_ref.shape[-1]
    lead = slope_ref.shape[0]
    is_last = lax.axis_index("ctx") == lax.axis_size("ctx") - 1
    mean, inv = moments(stats_ref, parcel_ref, members)
    sums = sums_ref[0:2] + whole(after_ref)
    mean_grad = sums[0:1] / members
    mean_cross = sums[1:2] / members
    for frame in range(frames):
        standard = (clip_ref[frame].reshape(-1, width).astype(f32) - mean) * inv
        shortcut = back_dot(cot_ref[frame].reshape(-1, out_width), short_ref[...])
        grad = grad_ref[frame]
        at = frame - (frames - lead)
        if at >= 0:
            following = after_ref[at * places : (at + 1) * places].astype(f32) * slope_ref[at]
            grad = grad + jnp.where(is_last, 0.0, following)
        grad = (grad - mean_grad - standard * mean_cross) * inv + shortcut
        out_ref[frame] = grad.astype(bf16).reshape(rows, cols, width)


def first_kernel(total_ref, got_ref, keep_ref, *send_refs):
    at = lax.axis_index("dp")
    z, x, core = at // 4, lax.rem(at // 2, 2), lax.rem(at, 2)
    y = lax.axis_index("ctx")
    plane = x + 2 * y
    for step, target in enumerate((keep_ref, *send_refs)):
        for inner in range(4):
            to_plane = jnp.where(core == 0, lax.bitwise_xor(plane, step), inner)
            to_z = jnp.where(core == 0, inner, lax.bitwise_xor(z, step))
            to_x, to_y = lax.rem(to_plane, 2), to_plane // 2
            value = total_ref[to_y, to_z, to_x, core] + got_ref[to_y, to_z, to_x].astype(f32)
            target[inner] = value.astype(target.dtype)


def second_kernel(keep_ref, a_ref, b_ref, c_ref, own_ref, *send_refs):
    at = lax.axis_index("dp")
    plane = lax.rem(at // 2, 2) + 2 * lax.axis_index("ctx")
    here = jnp.where(lax.rem(at, 2) == 0, at // 4, plane)
    for step, target in enumerate((own_ref, *send_refs)):
        to = lax.bitwise_xor(here, step)
        value = keep_ref[to] + a_ref[to].astype(f32) + (b_ref[to].astype(f32) + c_ref[to].astype(f32))
        target[...] = value.astype(target.dtype)


def last_kernel(scale, own_ref, a_ref, b_ref, c_ref, conv_ref, short_ref):
    value = own_ref[...] + a_ref[...].astype(f32) + (b_ref[...].astype(f32) + c_ref[...].astype(f32))
    value = value * scale
    conv_ref[...] = value[: conv_ref.shape[0]]
    short_ref[...] = value[conv_ref.shape[0] :]


def from_behind(value, axis, steps):
    count = lax.axis_size(axis)
    initial, last = (max(0, -steps), min(count, count - steps))
    return lax.ppermute(value, axis, [(source, source + steps) for source in range(initial, last)])


def others_total(value):
    count = lax.axis_size("ctx")
    total = None
    for step in range(1, count):
        got = lax.ppermute(value, "ctx", [(source, (source + step) % count) for source in range(count)])
        total = got if total is None else total + got
    return jnp.zeros_like(value) if total is None else total


def swap(value, core_0, core_1):
    dp, ctx = lax.axis_size("dp"), lax.axis_size("ctx")
    masks = (core_0, core_1)
    pairs = []
    for source in range(dp * ctx):
        at, side = divmod(source, ctx)
        dp_mask, ctx_mask = masks[at % 2]
        pairs.append((source, (at ^ dp_mask) * ctx + (side ^ ctx_mask)))
    return lax.ppermute(value, ("dp", "ctx"), pairs)


def exchange(sends, plane_core):
    got = []
    for step in (3, 2, 1):
        masks = [None, None]
        masks[plane_core] = (2 * (step % 2), step // 2)
        masks[1 - plane_core] = (4 * step, 0)
        got.append(swap(sends[step - 1], *masks))
    return got


def sort_first(total, got):
    halves, blocks, rows, cols = got.shape
    part = (4, rows, cols)
    return call(
        first_kernel,
        [jax.ShapeDtypeStruct(part, f32)] + [jax.ShapeDtypeStruct(part, bf16)] * 3,
    )(total.reshape(halves, blocks // 2, 2, 2, rows, cols), got.reshape(halves, blocks // 2, 2, rows, cols))


def sort_second(keep, *got):
    part = keep.shape[1:]
    return call(
        second_kernel,
        [jax.ShapeDtypeStruct(part, f32)] + [jax.ShapeDtypeStruct(part, bf16)] * 3,
    )(keep, *got)


def add_last(mine, from_a, from_b, from_c, conv_rows, short_rows, scale):
    cols = mine.shape[1]
    return call(
        functools.partial(last_kernel, scale),
        [jax.ShapeDtypeStruct((conv_rows, cols), f32), jax.ShapeDtypeStruct((short_rows, cols), f32)],
        moved=mine.size * 12,
    )(mine, from_a, from_b, from_c)


def body(clip_in, norm_gain, norm_bias, conv_weight, short_weight, out_cotangent):
    batch_clips, frames, height, breadth, in_width = clip_in.shape
    assert batch_clips == 1
    out_width = conv_weight.shape[1]
    per_group = in_width // GROUPS
    dp_size, ctx_size = lax.axis_size("dp"), lax.axis_size("ctx")
    total_frames = frames * ctx_size
    members = total_frames * height * breadth * per_group
    scale = 1.0 / (batch_clips * dp_size * total_frames)
    places = frames * height * breadth
    clip = clip_in[0]
    cot = out_cotangent[0]
    gain = norm_gain.reshape(1, in_width)
    bias = norm_bias.reshape(1, in_width)
    conv_all = TAPS * in_width
    work = places * conv_all * out_width * 2

    lead = KT - 1
    stats, parcel = call(
        start_kernel,
        [
            jax.ShapeDtypeStruct((8, in_width), f32),
            jax.ShapeDtypeStruct((lead * height * breadth + 16, in_width), bf16),
        ],
        flops=work, moved=clip.size * 2,
    )(clip)
    if ctx_size == 2:
        before = lax.ppermute(parcel, "ctx", [(0, 1), (1, 0)])
    else:
        before = from_behind(clip[frames - lead :], "ctx", 1).reshape(-1, in_width)
        before = jnp.concatenate([before, pieces_block(others_total(stats))], axis=0)

    back_part, leading, cot_t = call(
        back_kernel,
        [
            jax.ShapeDtypeStruct((frames, height * breadth, in_width), f32),
            jax.ShapeDtypeStruct((lead, height * breadth, in_width), bf16),
            jax.ShapeDtypeStruct((out_width, places), bf16),
        ],
        [pltpu.VMEM((KS, frames, height + 2, breadth, out_width), bf16)],
        flops=2 * work, moved=conv_weight.size * 2,
    )(cot, conv_weight)
    before, back_part = lax.optimization_barrier((before, back_part))

    staged = dp_size == 16 and ctx_size == 2
    conv_rows, short_rows = conv_all // dp_size, in_width // dp_size
    if staged:
        cols = out_width // ctx_size
        block = (conv_rows + short_rows, cols)
        outs = [
            jax.ShapeDtypeStruct((ctx_size, dp_size) + block, f32),
            jax.ShapeDtypeStruct((ctx_size, dp_size // 2) + block, bf16),
        ]
        split = (conv_rows, short_rows, conv_all)
    else:
        outs = [jax.ShapeDtypeStruct((conv_all + in_width, out_width), f32)]
        split = None
    hidden, *parts = call(
        functools.partial(weight_kernel, members, split),
        [jax.ShapeDtypeStruct((KS, frames + lead, height + 2, breadth, in_width), bf16)] + outs,
        flops=work, moved=cot.size * 2,
    )(clip, before, stats, gain, bias, cot_t)

    clip_out = forward_half(0, hidden, clip, conv_weight, short_weight)
    if staged:
        got, clip_out = lax.optimization_barrier((swap(parts[1], (1, 0), (1, 0)), clip_out))
        keep, *sends = sort_first(parts[0], got)
        got = exchange(sends, 0)
        hidden, keep = lax.optimization_barrier((hidden, keep))
    clip_out = forward_half(1, hidden, clip, conv_weight, short_weight, clip_out)
    leading, clip_out = lax.optimization_barrier((leading, clip_out))
    parcel_shape = jax.ShapeDtypeStruct((lead * height * breadth + 16, in_width), bf16)
    grad, slope, sums, parcel = call(
        functools.partial(activation_kernel, members),
        [
            jax.ShapeDtypeStruct((frames, height * breadth, in_width), f32),
            jax.ShapeDtypeStruct((lead, height * breadth, in_width), f32),
            jax.ShapeDtypeStruct((8, in_width), f32),
            parcel_shape,
        ],
    )(back_part, leading, clip, before, stats, gain, bias)
    if ctx_size == 2:
        after = lax.ppermute(parcel, "ctx", [(0, 1), (1, 0)])
    else:
        after = from_behind(leading, "ctx", -1).reshape(-1, in_width)
        after = jnp.concatenate([after, pieces_block(others_total(sums))], axis=0)
    if staged:
        *got, sums = lax.optimization_barrier((*got, sums))
        mine, *sends = sort_second(keep, *got)
        got = exchange(sends, 1)
        conv_grad, short_grad = add_last(mine, *got, conv_rows, short_rows, scale)
        after, mine = lax.optimization_barrier((after, mine))
    else:
        summed = []
        for part in (parts[0][:conv_all], parts[0][conv_all:]):
            part = lax.psum_scatter(part, "dp", scatter_dimension=0, tiled=True)
            part = lax.psum_scatter(part, "ctx", scatter_dimension=1, tiled=True)
            summed.append(part * scale)
        conv_grad, short_grad = summed
    clip_grad = call(
        functools.partial(finish_kernel, members),
        jax.ShapeDtypeStruct((frames, height, breadth, in_width), bf16),
        flops=work // 20, moved=cot.size * 4,
    )(grad, slope, sums, after, clip, before, stats, cot, short_weight)
    return (clip_out[None], clip_grad[None], conv_grad, short_grad)


def solution(mesh):
    return jax.shard_map(
        body,
        mesh=mesh,
        in_specs=(
            P("dp", "ctx", None, None, None),
            P(),
            P(),
            P(),
            P(),
            P("dp", "ctx", None, None, None),
        ),
        out_specs=(
            P("dp", "ctx", None, None, None),
            P("dp", "ctx", None, None, None),
            P("dp", "ctx"),
            P("dp", "ctx"),
        ),
        check_vma=False,
    )
```

```python
import functools

import jax
import jax.numpy as jnp
from jax import lax
from jax.experimental import pallas as pl
from jax.experimental.pallas import tpu as pltpu
from jax.sharding import PartitionSpec as P

GROUPS = 32
KT = 3
KS = 3
TAPS = KT * KS * KS
VMEM_BYTES = 28 * 1024 * 1024

epsilon = 1e-06
f32 = jnp.float32
bf16 = jnp.bfloat16


def call(kernel, outs, scratch=(), flops=0, moved=0, in_specs=None, out_specs=None, aliases=None):
    specs = {} if in_specs is None else {"in_specs": in_specs}
    if out_specs is not None:
        specs.update(out_specs=out_specs, input_output_aliases=aliases)
    return pl.pallas_call(
        kernel,
        out_shape=outs,
        **specs,
        scratch_shapes=list(scratch),
        compiler_params=pltpu.CompilerParams(vmem_limit_bytes=VMEM_BYTES),
        cost_estimate=pl.CostEstimate(flops=flops, bytes_accessed=moved, transcendentals=0),
    )


def group_totals(rows):
    width = rows.shape[1]
    per_group = width // GROUPS
    row = lax.broadcasted_iota(jnp.int32, (width, width), 0) // per_group
    col = lax.broadcasted_iota(jnp.int32, (width, width), 1) // per_group
    same = (row == col).astype(f32)
    return lax.dot_general(
        rows, same, (((1,), (0,)), ((), ())), precision=lax.Precision.HIGHEST, preferred_element_type=f32
    )


def two_rows(first, second):
    at = lax.broadcasted_iota(jnp.int32, (8, first.shape[1]), 0)
    return jnp.where(at == 0, first, jnp.where(at == 1, second, 0.0))


def column_totals(value):
    return jnp.sum(value, axis=0, keepdims=True)


def in_pieces(value):
    high = value.astype(bf16)
    rest = value - high.astype(f32)
    middle = rest.astype(bf16)
    low = (rest - middle.astype(f32)).astype(bf16)
    return high, middle, low


def pieces_block(totals):
    pieces = [piece[0:2].astype(f32) for piece in in_pieces(totals)]
    zero = jnp.zeros((10, totals.shape[1]), f32)
    return jnp.concatenate(pieces + [zero], axis=0).astype(bf16)


def start_kernel(clip_ref, stats_ref, parcel_ref):
    frames, rows, cols, width = clip_ref.shape
    places = rows * cols
    total = jnp.zeros((1, width), f32)
    square = jnp.zeros((1, width), f32)
    for frame in range(frames):
        value = clip_ref[frame].reshape(-1, width).astype(f32)
        total = total + column_totals(value)
        square = square + column_totals(value * value)
    totals = group_totals(two_rows(total, square))
    stats_ref[...] = totals
    lead = KT - 1
    for frame in range(lead):
        parcel_ref[frame * places : (frame + 1) * places] = clip_ref[frames - lead + frame].reshape(places, width)
    parcel_ref[lead * places :] = pieces_block(totals)


def whole(parcel):
    pieces = parcel[parcel.shape[0] - 16 :].astype(f32)
    return pieces[0:2] + (pieces[2:4] + pieces[4:6])


def moments(stats, parcel, members):
    totals = stats[0:2] + whole(parcel)
    mean = totals[0:1] / members
    variance = totals[1:2] / members - mean * mean
    return mean, lax.rsqrt(variance + epsilon)


def shift_columns(value, step):
    rows, cols, width = value.shape
    flat = value.reshape(rows * cols, width)
    rolled = pltpu.roll(flat, (-step) % (rows * cols), 0).reshape(rows, cols, width)
    at = lax.broadcasted_iota(jnp.int32, (rows, cols, width), 1)
    edge = cols - 1 if step == 1 else 0
    return jnp.where(at == edge, 0.0, rolled)


def place(padded, frame, value):
    rows, cols, width = value.shape
    for j, step in enumerate((-1, 0, 1)):
        moved = value if step == 0 else shift_columns(value, step)
        padded[j, frame, 1 : rows + 1] = moved.astype(bf16)


def clear_edges(padded):
    rows = padded.shape[2]
    zero = jnp.zeros(padded.shape[:2] + padded.shape[3:], bf16)
    padded[:, :, 0] = zero
    padded[:, :, rows - 1] = zero


def hidden_of(value, mean, inv, gain, bias):
    affine = (value.astype(f32) - mean) * inv * gain + bias
    return affine * jax.nn.sigmoid(affine)


def fill_hidden(padded, clip_ref, parcel_ref, mean, inv, gain, bias, begin, stop):
    frames, rows, cols, width = clip_ref.shape
    places = rows * cols
    lead = KT - 1
    at_start = lax.axis_index("ctx") == 0
    for frame in range(begin, stop):
        if frame < lead:
            before = parcel_ref[frame * places : (frame + 1) * places].reshape(rows, cols, width)
            value = jnp.where(at_start, clip_ref[0].astype(f32), before.astype(f32))
        else:
            value = clip_ref[frame - lead].astype(f32)
        place(padded, frame, hidden_of(value, mean, inv, gain, bias))


def tap_block(padded, frames, rows, t, i):
    width = padded.shape[-1]
    return [padded[j, t : t + frames, i : i + rows].reshape(-1, width) for j in range(KS)]


def weight_kernel(
    members, split,
    clip_ref, parcel_ref, stats_ref, gain_ref, bias_ref, cot_t_ref,
    padded, total, *rest,
):
    frames, rows, cols, width = clip_ref.shape
    mean, inv = moments(stats_ref, parcel_ref, members)
    clear_edges(padded)
    filled = 0
    cot_t = cot_t_ref[...]
    pieces = [(t, i) for t in range(KT) for i in range(KS)]
    begin = 0
    for at in range(0, len(pieces), 2):
        parts = []
        needed = pieces[at : at + 2][-1][0] + frames
        fill_hidden(padded, clip_ref, parcel_ref, mean, inv, gain_ref[...], bias_ref[...], filled, needed)
        filled = needed
        for t, i in pieces[at : at + 2]:
            parts += tap_block(padded, frames, rows, t, i)
        if at + 2 > len(pieces):
            parts.append(clip_ref[...].reshape(-1, width))
        part = jnp.dot(cot_t, jnp.concatenate(parts, axis=1), preferred_element_type=f32).T
        if split is None:
            total[begin : begin + part.shape[0], :] = part
        else:
            scatter_rows(total, part, begin, split)
        begin += part.shape[0]
    if split is not None:
        (send_ref,) = rest
        core = lax.rem(lax.axis_index("dp"), 2)
        halves, blocks = send_ref.shape[:2]
        for half in range(halves):
            for k in range(blocks):
                send_ref[half, k] = total[half, 2 * k + 1 - core].astype(bf16)


def scatter_rows(total, part, begin, split):
    conv_rows, short_rows, conv_all = split
    halves = total.shape[0]
    row, stop = begin, begin + part.shape[0]
    width = total.shape[-1]
    while row < stop:
        if row < conv_all:
            block, offset = divmod(row, conv_rows)
            count = min(conv_rows - offset, stop - row, conv_all - row)
            target = offset
        else:
            block, offset = divmod(row - conv_all, short_rows)
            count = min(short_rows - offset, stop - row)
            target = conv_rows + offset
        for half in range(halves):
            total[half, block, target : target + count, :] = part[
                row - begin : row - begin + count, half * width : (half + 1) * width
            ]
        row += count


def forward_kernel(begin, padded, clip_ref, weight_ref, short_ref, *rest):
    out_ref = rest[-1]
    rows, cols, width = clip_ref.shape[1:]
    for at in range(out_ref.shape[0]):
        frame = begin + at
        parts = []
        for t in range(KT):
            for i in range(KS):
                for j in range(KS):
                    parts.append(padded[j, frame + t, i : i + rows].reshape(-1, width))
        result = jnp.dot(jnp.concatenate(parts, axis=1), weight_ref[...], preferred_element_type=f32)
        result = result + jnp.dot(
            clip_ref[frame].reshape(-1, width), short_ref[...], preferred_element_type=f32
        )
        out_ref[at] = result.astype(bf16).reshape(rows, cols, -1)


def forward_half(half, hidden, clip, conv_weight, short_weight, whole_shape=False):
    frames, height, breadth, _ = clip.shape
    out_width = conv_weight.shape[1]
    count = frames // 2
    flops = 2 * conv_weight.size * count * height * breadth
    vmem = pl.BlockSpec(memory_space=pltpu.VMEM)
    block = (count, height, breadth, out_width)
    at = half if whole_shape else 0
    return pl.pallas_call(
        functools.partial(forward_kernel, half * count),
        out_shape=jax.ShapeDtypeStruct((frames if whole_shape else count,) + block[1:], bf16),
        grid=(1,),
        in_specs=[vmem] * 4,
        out_specs=pl.BlockSpec(block, lambda step: (at, 0, 0, 0)),
        compiler_params=pltpu.CompilerParams(vmem_limit_bytes=VMEM_BYTES),
        cost_estimate=pl.CostEstimate(flops=flops // 4, bytes_accessed=0, transcendentals=0),
    )(hidden, clip, conv_weight, short_weight)


def back_weights(weight_ref, width, taps_t):
    bands = []
    for t in taps_t:
        bands.append(
            jnp.concatenate(
                [weight_ref[(t * KS * KS + q) * width : (t * KS * KS + q + 1) * width, :] for q in range(KS * KS)],
                axis=1,
            )
        )
    return jnp.concatenate(bands, axis=0) if len(bands) > 1 else bands[0]


def fill_cot(padded, cot_ref):
    clear_edges(padded)
    for frame in range(cot_ref.shape[0]):
        place(padded, frame, cot_ref[frame].astype(f32))


def spatial_block(padded, frame, rows):
    out_width = padded.shape[-1]
    parts = []
    for i in range(KS):
        for j in range(KS):
            parts.append(padded[2 - j, frame, 2 - i : 2 - i + rows].reshape(-1, out_width))
    return jnp.concatenate(parts, axis=1)


def back_dot(block, weights):
    return lax.dot_general(block, weights, (((1,), (1,)), ((), ())), preferred_element_type=f32)


def back_kernel(cot_ref, weight_ref, out_ref, before_ref, cot_t_ref, padded):
    frames, rows, cols, out_width = cot_ref.shape
    width = out_ref.shape[-1]
    at_start = lax.axis_index("ctx") == 0
    cot_t_ref[...] = cot_ref[...].reshape(-1, out_width).T
    fill_cot(padded, cot_ref)
    late = back_weights(weight_ref, width, (2, 1))
    early = back_weights(weight_ref, width, (0,))
    for frame in range(frames):
        block = spatial_block(padded, frame, rows)
        both = back_dot(block, late)
        y2, y1 = both[:, :width], both[:, width:]
        y0 = back_dot(block, early)
        if frame == 0:
            lead, next_lead = y0, y1
            out_ref[0] = y2
        else:
            out_ref[frame] = y2
            out_ref[frame - 1] += y1
            if frame == 1:
                next_lead = next_lead + y0
                before_ref[0] = lead.astype(bf16)
                before_ref[1] = next_lead.astype(bf16)
                out_ref[0] += jnp.where(at_start, lead + next_lead, 0.0)
            else:
                out_ref[frame - 2] += y0


def activation_kernel(
    members,
    part_ref, leading_ref, clip_ref, parcel_ref, stats_ref, gain_ref, bias_ref, half_ref, _,
    grad_ref, slope_ref, sums_ref, out_ref, whole_ref, sem,
):
    count = half_ref.shape[0]
    copy = pltpu.make_async_copy(half_ref, whole_ref.at[pl.ds(whole_ref.shape[0] - count, count)], sem)
    copy.start()
    frames, rows, cols, width = clip_ref.shape
    places = rows * cols
    gain = gain_ref[...]
    mean, inv = moments(stats_ref, parcel_ref, members)

    def standard_and_slope(value):
        standard = (value.astype(f32) - mean) * inv
        affine = standard * gain + bias_ref[...]
        logistic = jax.nn.sigmoid(affine)
        return standard, logistic * (1.0 + affine * (1.0 - logistic)) * gain

    total = jnp.zeros((1, width), f32)
    cross = jnp.zeros((1, width), f32)
    lead = leading_ref.shape[0]
    for frame in range(lead):
        here = slice(frame * places, (frame + 1) * places)
        standard, slope = standard_and_slope(parcel_ref[here])
        grad = leading_ref[frame].astype(f32) * slope
        total = total + column_totals(grad)
        cross = cross + column_totals(grad * standard)
        out_ref[here] = leading_ref[frame]
    at_start = lax.axis_index("ctx") == 0
    total = jnp.where(at_start, 0.0, total)
    cross = jnp.where(at_start, 0.0, cross)
    for frame in range(frames):
        standard, slope = standard_and_slope(clip_ref[frame].reshape(-1, width))
        grad = part_ref[frame] * slope
        grad_ref[frame] = grad
        if frame >= frames - lead:
            slope_ref[frame - (frames - lead)] = slope
        total = total + column_totals(grad)
        cross = cross + column_totals(grad * standard)
    sums = group_totals(two_rows(total, cross))
    sums_ref[...] = sums
    out_ref[lead * places :] = pieces_block(sums)
    copy.wait()


def finish_kernel(
    members,
    grad_ref, slope_ref, sums_ref, after_ref, clip_ref, parcel_ref, stats_ref, cot_ref, short_ref,
    out_ref,
):
    frames, rows, cols, width = clip_ref.shape
    places = rows * cols
    out_width = cot_ref.shape[-1]
    lead = slope_ref.shape[0]
    is_last = lax.axis_index("ctx") == lax.axis_size("ctx") - 1
    mean, inv = moments(stats_ref, parcel_ref, members)
    sums = sums_ref[0:2] + whole(after_ref)
    mean_grad = sums[0:1] / members
    mean_cross = sums[1:2] / members
    for frame in range(frames):
        standard = (clip_ref[frame].reshape(-1, width).astype(f32) - mean) * inv
        shortcut = back_dot(cot_ref[frame].reshape(-1, out_width), short_ref[...])
        grad = grad_ref[frame]
        at = frame - (frames - lead)
        if at >= 0:
            following = after_ref[at * places : (at + 1) * places].astype(f32) * slope_ref[at]
            grad = grad + jnp.where(is_last, 0.0, following)
        grad = (grad - mean_grad - standard * mean_cross) * inv + shortcut
        out_ref[frame] = grad.astype(bf16).reshape(rows, cols, width)


def first_kernel(total_ref, got_ref, keep_ref, *send_refs):
    at = lax.axis_index("dp")
    z, x, core = at // 4, lax.rem(at // 2, 2), lax.rem(at, 2)
    y = lax.axis_index("ctx")
    plane = x + 2 * y
    for step, target in enumerate((keep_ref, *send_refs)):
        for inner in range(4):
            to_plane = jnp.where(core == 0, lax.bitwise_xor(plane, step), inner)
            to_z = jnp.where(core == 0, inner, lax.bitwise_xor(z, step))
            to_x, to_y = lax.rem(to_plane, 2), to_plane // 2
            value = total_ref[to_y, to_z, to_x, core] + got_ref[to_y, to_z, to_x].astype(f32)
            target[inner] = value.astype(target.dtype)


def second_kernel(keep_ref, a_ref, b_ref, c_ref, own_ref, *send_refs):
    at = lax.axis_index("dp")
    plane = lax.rem(at // 2, 2) + 2 * lax.axis_index("ctx")
    here = jnp.where(lax.rem(at, 2) == 0, at // 4, plane)
    for step, target in enumerate((own_ref, *send_refs)):
        to = lax.bitwise_xor(here, step)
        value = keep_ref[to] + a_ref[to].astype(f32) + (b_ref[to].astype(f32) + c_ref[to].astype(f32))
        target[...] = value.astype(target.dtype)


def last_kernel(scale, own_ref, a_ref, b_ref, c_ref, conv_ref, short_ref):
    value = own_ref[...] + a_ref[...].astype(f32) + (b_ref[...].astype(f32) + c_ref[...].astype(f32))
    value = value * scale
    conv_ref[...] = value[: conv_ref.shape[0]]
    short_ref[...] = value[conv_ref.shape[0] :]


def from_behind(value, axis, steps):
    count = lax.axis_size(axis)
    initial, last = (max(0, -steps), min(count, count - steps))
    return lax.ppermute(value, axis, [(source, source + steps) for source in range(initial, last)])


def others_total(value):
    count = lax.axis_size("ctx")
    total = None
    for step in range(1, count):
        got = lax.ppermute(value, "ctx", [(source, (source + step) % count) for source in range(count)])
        total = got if total is None else total + got
    return jnp.zeros_like(value) if total is None else total


def swap(value, core_0, core_1):
    dp, ctx = lax.axis_size("dp"), lax.axis_size("ctx")
    masks = (core_0, core_1)
    pairs = []
    for source in range(dp * ctx):
        at, side = divmod(source, ctx)
        dp_mask, ctx_mask = masks[at % 2]
        pairs.append((source, (at ^ dp_mask) * ctx + (side ^ ctx_mask)))
    return lax.ppermute(value, ("dp", "ctx"), pairs)


def exchange(sends, plane_core):
    got = []
    for step in (3, 2, 1):
        masks = [None, None]
        masks[plane_core] = (2 * (step % 2), step // 2)
        masks[1 - plane_core] = (4 * step, 0)
        got.append(swap(sends[step - 1], *masks))
    return got


def sort_first(total, got):
    halves, blocks, rows, cols = got.shape
    part = (4, rows, cols)
    return call(
        first_kernel,
        [jax.ShapeDtypeStruct(part, f32)] + [jax.ShapeDtypeStruct(part, bf16)] * 3,
    )(total.reshape(halves, blocks // 2, 2, 2, rows, cols), got.reshape(halves, blocks // 2, 2, rows, cols))


def sort_second(keep, *got):
    part = keep.shape[1:]
    return call(
        second_kernel,
        [jax.ShapeDtypeStruct(part, f32)] + [jax.ShapeDtypeStruct(part, bf16)] * 3,
    )(keep, *got)


def add_last(mine, from_a, from_b, from_c, conv_rows, short_rows, scale):
    cols = mine.shape[1]
    return call(
        functools.partial(last_kernel, scale),
        [jax.ShapeDtypeStruct((conv_rows, cols), f32), jax.ShapeDtypeStruct((short_rows, cols), f32)],
        moved=mine.size * 12,
    )(mine, from_a, from_b, from_c)


def body(clip_in, norm_gain, norm_bias, conv_weight, short_weight, out_cotangent):
    batch_clips, frames, height, breadth, in_width = clip_in.shape
    assert batch_clips == 1
    out_width = conv_weight.shape[1]
    per_group = in_width // GROUPS
    dp_size, ctx_size = lax.axis_size("dp"), lax.axis_size("ctx")
    total_frames = frames * ctx_size
    members = total_frames * height * breadth * per_group
    scale = 1.0 / (batch_clips * dp_size * total_frames)
    places = frames * height * breadth
    clip = clip_in[0]
    cot = out_cotangent[0]
    gain = norm_gain.reshape(1, in_width)
    bias = norm_bias.reshape(1, in_width)
    conv_all = TAPS * in_width
    work = places * conv_all * out_width * 2

    lead = KT - 1
    stats, parcel = call(
        start_kernel,
        [
            jax.ShapeDtypeStruct((8, in_width), f32),
            jax.ShapeDtypeStruct((lead * height * breadth + 16, in_width), bf16),
        ],
        flops=work, moved=clip.size * 2,
    )(clip)
    if ctx_size == 2:
        before = lax.ppermute(parcel, "ctx", [(0, 1), (1, 0)])
    else:
        before = from_behind(clip[frames - lead :], "ctx", 1).reshape(-1, in_width)
        before = jnp.concatenate([before, pieces_block(others_total(stats))], axis=0)

    back_part, leading, cot_t = call(
        back_kernel,
        [
            jax.ShapeDtypeStruct((frames, height * breadth, in_width), f32),
            jax.ShapeDtypeStruct((lead, height * breadth, in_width), bf16),
            jax.ShapeDtypeStruct((out_width, places), bf16),
        ],
        [pltpu.VMEM((KS, frames, height + 2, breadth, out_width), bf16)],
        flops=2 * work, moved=conv_weight.size * 2,
    )(cot, conv_weight)
    before, back_part = lax.optimization_barrier((before, back_part))

    staged = dp_size == 16 and ctx_size == 2
    conv_rows, short_rows = conv_all // dp_size, in_width // dp_size
    if staged:
        cols = out_width // ctx_size
        block = (conv_rows + short_rows, cols)
        outs = [
            jax.ShapeDtypeStruct((ctx_size, dp_size) + block, f32),
            jax.ShapeDtypeStruct((ctx_size, dp_size // 2) + block, bf16),
        ]
        split = (conv_rows, short_rows, conv_all)
    else:
        outs = [jax.ShapeDtypeStruct((conv_all + in_width, out_width), f32)]
        split = None
    hidden, *parts = call(
        functools.partial(weight_kernel, members, split),
        [jax.ShapeDtypeStruct((KS, frames + lead, height + 2, breadth, in_width), bf16)] + outs,
        flops=work, moved=cot.size * 2,
    )(clip, before, stats, gain, bias, cot_t)

    clip_out = forward_half(0, hidden, clip, conv_weight, short_weight, True)
    if staged:
        got, clip_out = lax.optimization_barrier((swap(parts[1], (1, 0), (1, 0)), clip_out))
        keep, *sends = sort_first(parts[0], got)
        got = exchange(sends, 0)
        hidden, keep = lax.optimization_barrier((hidden, keep))
    second_half = forward_half(1, hidden, clip, conv_weight, short_weight)
    anywhere, vmem = pl.BlockSpec(memory_space=pl.ANY), pl.BlockSpec(memory_space=pltpu.VMEM)
    parcel_shape = jax.ShapeDtypeStruct((lead * height * breadth + 16, in_width), bf16)
    grad, slope, sums, parcel, clip_out = call(
        functools.partial(activation_kernel, members),
        [
            jax.ShapeDtypeStruct((frames, height * breadth, in_width), f32),
            jax.ShapeDtypeStruct((lead, height * breadth, in_width), f32),
            jax.ShapeDtypeStruct((8, in_width), f32),
            parcel_shape,
            jax.ShapeDtypeStruct(clip_out.shape, bf16),
        ],
        [pltpu.SemaphoreType.DMA],
        in_specs=[vmem] * 8 + [anywhere],
        out_specs=[vmem] * 4 + [anywhere],
        aliases={8: 4},
    )(back_part, leading, clip, before, stats, gain, bias, second_half, clip_out)
    if ctx_size == 2:
        after = lax.ppermute(parcel, "ctx", [(0, 1), (1, 0)])
    else:
        after = from_behind(leading, "ctx", -1).reshape(-1, in_width)
        after = jnp.concatenate([after, pieces_block(others_total(sums))], axis=0)
    if staged:
        *got, sums = lax.optimization_barrier((*got, sums))
        mine, *sends = sort_second(keep, *got)
        got = exchange(sends, 1)
        conv_grad, short_grad = add_last(mine, *got, conv_rows, short_rows, scale)
        after, mine = lax.optimization_barrier((after, mine))
    else:
        summed = []
        for part in (parts[0][:conv_all], parts[0][conv_all:]):
            part = lax.psum_scatter(part, "dp", scatter_dimension=0, tiled=True)
            part = lax.psum_scatter(part, "ctx", scatter_dimension=1, tiled=True)
            summed.append(part * scale)
        conv_grad, short_grad = summed
    clip_grad = call(
        functools.partial(finish_kernel, members),
        jax.ShapeDtypeStruct((frames, height, breadth, in_width), bf16),
        flops=work // 20, moved=cot.size * 4,
    )(grad, slope, sums, after, clip, before, stats, cot, short_weight)
    return (clip_out[None], clip_grad[None], conv_grad, short_grad)


def solution(mesh):
    return jax.shard_map(
        body,
        mesh=mesh,
        in_specs=(
            P("dp", "ctx", None, None, None),
            P(),
            P(),
            P(),
            P(),
            P("dp", "ctx", None, None, None),
        ),
        out_specs=(
            P("dp", "ctx", None, None, None),
            P("dp", "ctx", None, None, None),
            P("dp", "ctx"),
            P("dp", "ctx"),
        ),
        check_vma=False,
    )
```

```python
import functools

import jax
import jax.numpy as jnp
from jax import lax
from jax.experimental import pallas as pl
from jax.experimental.pallas import tpu as pltpu
from jax.sharding import PartitionSpec as P

GROUPS = 32
KT = 3
KS = 3
TAPS = KT * KS * KS
VMEM_BYTES = 28 * 1024 * 1024

epsilon = 1e-06
f32 = jnp.float32
bf16 = jnp.bfloat16


def call(kernel, outs, scratch=(), flops=0, moved=0, in_specs=None, out_specs=None):
    specs = {} if in_specs is None else {"in_specs": in_specs}
    if out_specs is not None:
        specs["out_specs"] = out_specs
    return pl.pallas_call(
        kernel,
        out_shape=outs,
        **specs,
        scratch_shapes=list(scratch),
        compiler_params=pltpu.CompilerParams(vmem_limit_bytes=VMEM_BYTES),
        cost_estimate=pl.CostEstimate(flops=flops, bytes_accessed=moved, transcendentals=0),
    )


def group_totals(rows):
    width = rows.shape[1]
    per_group = width // GROUPS
    row = lax.broadcasted_iota(jnp.int32, (width, width), 0) // per_group
    col = lax.broadcasted_iota(jnp.int32, (width, width), 1) // per_group
    same = (row == col).astype(f32)
    return lax.dot_general(
        rows, same, (((1,), (0,)), ((), ())), precision=lax.Precision.HIGHEST, preferred_element_type=f32
    )


def two_rows(first, second):
    at = lax.broadcasted_iota(jnp.int32, (8, first.shape[1]), 0)
    return jnp.where(at == 0, first, jnp.where(at == 1, second, 0.0))


def column_totals(value):
    return jnp.sum(value, axis=0, keepdims=True)


def in_pieces(value):
    high = value.astype(bf16)
    rest = value - high.astype(f32)
    middle = rest.astype(bf16)
    low = (rest - middle.astype(f32)).astype(bf16)
    return high, middle, low


def pieces_block(totals):
    pieces = [piece[0:2].astype(f32) for piece in in_pieces(totals)]
    zero = jnp.zeros((10, totals.shape[1]), f32)
    return jnp.concatenate(pieces + [zero], axis=0).astype(bf16)


def start_kernel(clip_ref, stats_ref, last_ref):
    frames = clip_ref.shape[0]
    width = clip_ref.shape[-1]
    total = jnp.zeros((1, width), f32)
    square = jnp.zeros((1, width), f32)
    for frame in range(frames):
        value = clip_ref[frame].reshape(-1, width).astype(f32)
        total = total + column_totals(value)
        square = square + column_totals(value * value)
    stats_ref[...] = group_totals(two_rows(total, square))
    last_ref[...] = clip_ref[frames - last_ref.shape[0] :]


def whole(parcel):
    pieces = parcel[parcel.shape[0] - 16 :].astype(f32)
    return pieces[0:2] + (pieces[2:4] + pieces[4:6])


def moments(stats, other, members):
    totals = stats[0:2] + other[0:2]
    mean = totals[0:1] / members
    variance = totals[1:2] / members - mean * mean
    return mean, lax.rsqrt(variance + epsilon)


def shift_columns(value, step):
    rows, cols, width = value.shape
    flat = value.reshape(rows * cols, width)
    rolled = pltpu.roll(flat, (-step) % (rows * cols), 0).reshape(rows, cols, width)
    at = lax.broadcasted_iota(jnp.int32, (rows, cols, width), 1)
    edge = cols - 1 if step == 1 else 0
    return jnp.where(at == edge, 0.0, rolled)


def place(padded, frame, value):
    rows, cols, width = value.shape
    for j, step in enumerate((-1, 0, 1)):
        moved = value if step == 0 else shift_columns(value, step)
        padded[j, frame, 1 : rows + 1] = moved.astype(bf16)


def clear_edges(padded):
    rows = padded.shape[2]
    zero = jnp.zeros(padded.shape[:2] + padded.shape[3:], bf16)
    padded[:, :, 0] = zero
    padded[:, :, rows - 1] = zero


def hidden_of(value, mean, inv, gain, bias):
    affine = (value.astype(f32) - mean) * inv * gain + bias
    return affine * jax.nn.sigmoid(affine)


def tap_block(padded, frames, rows, t, i):
    width = padded.shape[-1]
    return [padded[j, t : t + frames, i : i + rows].reshape(-1, width) for j in range(KS)]


def groups_of_taps():
    return ((0, 1), (2,))


def weight_own_kernel(
    members,
    clip_ref, stats_ref, other_ref, gain_ref, bias_ref, cot_t_ref,
    padded, early_ref, late_ref,
):
    frames, rows, cols, width = clip_ref.shape
    mean, inv = moments(stats_ref, other_ref, members)
    clear_edges(padded)
    for frame in range(frames):
        place(padded, frame, hidden_of(clip_ref[frame], mean, inv, gain_ref[...], bias_ref[...]))
    per_frame = rows * cols
    for t in range(KT - 1, -1, -1):
        skipped = KT - 1 - t
        cot_t = cot_t_ref[:, skipped * per_frame :]
        base = row = t * KS * KS * width
        for group in groups_of_taps():
            parts = []
            for i in group:
                parts += tap_block(padded, frames - skipped, rows, 0, i)
            if t == KT - 1 and group[-1] == KS - 1:
                parts.append(clip_ref[...].reshape(-1, width))
            part = jnp.dot(cot_t, jnp.concatenate(parts, axis=1), preferred_element_type=f32)
            stop = row + part.shape[1]
            if t == KT - 1:
                late_ref[row - base : stop - base, :] = part.T
            else:
                early_ref[:, row:stop] = part
            row = stop


def weight_halo_kernel(
    members, split,
    halo_ref, clip_ref, stats_ref, other_ref, gain_ref, bias_ref, cot_t_ref, early_ref, late_ref,
    padded, total, *rest,
):
    at_start = lax.axis_index("ctx") == 0
    lead, rows, cols, width = halo_ref.shape
    mean, inv = moments(stats_ref, other_ref, members)
    clear_edges(padded)
    for frame in range(lead):
        value = jnp.where(at_start, clip_ref[0].astype(f32), halo_ref[frame].astype(f32))
        place(padded, frame, hidden_of(value, mean, inv, gain_ref[...], bias_ref[...]))
    per_frame = rows * cols

    def give(part, begin):
        if split is None:
            total[begin : begin + part.shape[0], :] = part
        else:
            scatter_rows(total, part, begin, split)

    give(late_ref[...], early_ref.shape[1])
    row = 0
    for t in range(KT - 1):
        count = lead - t
        for group in groups_of_taps():
            parts = []
            for i in group:
                parts += tap_block(padded, count, rows, t, i)
            part = jnp.dot(
                cot_t_ref[:, : count * per_frame], jnp.concatenate(parts, axis=1), preferred_element_type=f32
            )
            stop = row + part.shape[1]
            give((part + early_ref[:, row:stop]).T, row)
            row = stop
    if split is not None:
        (send_ref,) = rest
        core = lax.rem(lax.axis_index("dp"), 2)
        halves, blocks = send_ref.shape[:2]
        for half in range(halves):
            for k in range(blocks):
                send_ref[half, k] = total[half, 2 * k + 1 - core].astype(bf16)


def scatter_rows(total, part, begin, split):
    conv_rows, short_rows, conv_all = split
    halves = total.shape[0]
    row, stop = begin, begin + part.shape[0]
    width = total.shape[-1]
    while row < stop:
        if row < conv_all:
            block, offset = divmod(row, conv_rows)
            count = min(conv_rows - offset, stop - row, conv_all - row)
            target = offset
        else:
            block, offset = divmod(row - conv_all, short_rows)
            count = min(short_rows - offset, stop - row)
            target = conv_rows + offset
        for half in range(halves):
            total[half, block, target : target + count, :] = part[
                row - begin : row - begin + count, half * width : (half + 1) * width
            ]
        row += count


def forward_kernel(padded_lead, padded, clip_ref, weight_ref, short_ref, out_ref):
    frames, rows, cols, width = clip_ref.shape
    lead = padded_lead.shape[1]
    for frame in range(frames):
        parts = []
        for t in range(KT):
            source, at = (padded_lead, frame + t) if frame + t < lead else (padded, frame + t - lead)
            for i in range(KS):
                parts += tap_block(source, 1, rows, at, i)
        result = jnp.dot(jnp.concatenate(parts, axis=1), weight_ref[...], preferred_element_type=f32)
        result = result + jnp.dot(
            clip_ref[frame].reshape(-1, width), short_ref[...], preferred_element_type=f32
        )
        out_ref[frame] = result.astype(bf16).reshape(rows, cols, -1)


def back_weights(weight_ref, width, taps_t):
    bands = []
    for t in taps_t:
        bands.append(
            jnp.concatenate(
                [weight_ref[(t * KS * KS + q) * width : (t * KS * KS + q + 1) * width, :] for q in range(KS * KS)],
                axis=1,
            )
        )
    return jnp.concatenate(bands, axis=0) if len(bands) > 1 else bands[0]


def spatial_block(padded, frame, rows):
    out_width = padded.shape[-1]
    parts = []
    for i in range(KS):
        for j in range(KS):
            parts.append(padded[2 - j, frame, 2 - i : 2 - i + rows].reshape(-1, out_width))
    return jnp.concatenate(parts, axis=1)


def back_dot(block, weights):
    return lax.dot_general(block, weights, (((1,), (1,)), ((), ())), preferred_element_type=f32)


def back_products(begin, count, cot_ref, weight_ref, width, padded):
    rows, cols, out_width = cot_ref.shape[1:]
    clear_edges(padded)
    late = back_weights(weight_ref, width, (2, 1))
    early = back_weights(weight_ref, width, (0,))
    products = []
    for at in range(count):
        place(padded, at, cot_ref[begin + at].astype(f32))
        block = spatial_block(padded, at, rows)
        both = back_dot(block, late)
        products.append((both[:, :width], both[:, width:], back_dot(block, early)))
    return products


def back_first_kernel(cot_ref, weight_ref, out_ref, before_ref, cot_t_ref, padded):
    out_width = cot_ref.shape[-1]
    at_start = lax.axis_index("ctx") == 0
    cot_t_ref[...] = cot_ref[...].reshape(-1, out_width).T
    width = out_ref.shape[-1]
    (a2, a1, a0), (b2, b1, b0) = back_products(0, 2, cot_ref, weight_ref, width, padded)
    last = a1 + b0
    before_ref[0] = a0.astype(bf16)
    before_ref[1] = last.astype(bf16)
    out_ref[0] = a2 + b1 + jnp.where(at_start, a0 + last, 0.0)
    out_ref[1] = b2


def back_second_kernel(cot_ref, weight_ref, first_ref, out_ref, padded):
    width = out_ref.shape[-1]
    frames = cot_ref.shape[0]
    out_ref[0:2] = first_ref[...]
    for frame, (same, one, two) in enumerate(back_products(2, frames - 2, cot_ref, weight_ref, width, padded), 2):
        out_ref[frame] = same
        out_ref[frame - 1] += one
        out_ref[frame - 2] += two


def activation_kernel(
    members,
    part_ref, leading_ref, clip_ref, halo_ref, stats_ref, other_ref, gain_ref, bias_ref, forward_ref,
    grad_ref, slope_ref, sums_ref, out_ref, whole_ref, sem,
):
    copy = pltpu.make_async_copy(forward_ref, whole_ref, sem)
    copy.start()
    frames, rows, cols, width = clip_ref.shape
    places = rows * cols
    gain = gain_ref[...]
    mean, inv = moments(stats_ref, other_ref, members)

    def standard_and_slope(value):
        standard = (value.astype(f32) - mean) * inv
        affine = standard * gain + bias_ref[...]
        logistic = jax.nn.sigmoid(affine)
        return standard, logistic * (1.0 + affine * (1.0 - logistic)) * gain

    total = jnp.zeros((1, width), f32)
    cross = jnp.zeros((1, width), f32)
    lead = leading_ref.shape[0]
    for frame in range(lead):
        here = slice(frame * places, (frame + 1) * places)
        standard, slope = standard_and_slope(halo_ref[frame].reshape(-1, width))
        grad = leading_ref[frame].astype(f32) * slope
        total = total + column_totals(grad)
        cross = cross + column_totals(grad * standard)
        out_ref[here] = leading_ref[frame]
    at_start = lax.axis_index("ctx") == 0
    total = jnp.where(at_start, 0.0, total)
    cross = jnp.where(at_start, 0.0, cross)
    for frame in range(frames):
        standard, slope = standard_and_slope(clip_ref[frame].reshape(-1, width))
        grad = part_ref[frame] * slope
        grad_ref[frame] = grad
        if frame >= frames - lead:
            slope_ref[frame - (frames - lead)] = slope
        total = total + column_totals(grad)
        cross = cross + column_totals(grad * standard)
    sums = group_totals(two_rows(total, cross))
    sums_ref[...] = sums
    out_ref[lead * places :] = pieces_block(sums)
    copy.wait()


def finish_kernel(
    members,
    grad_ref, slope_ref, sums_ref, after_ref, clip_ref, stats_ref, other_ref, cot_ref, short_ref,
    out_ref,
):
    frames, rows, cols, width = clip_ref.shape
    places = rows * cols
    out_width = cot_ref.shape[-1]
    lead = slope_ref.shape[0]
    is_last = lax.axis_index("ctx") == lax.axis_size("ctx") - 1
    mean, inv = moments(stats_ref, other_ref, members)
    sums = sums_ref[0:2] + whole(after_ref)
    mean_grad = sums[0:1] / members
    mean_cross = sums[1:2] / members
    for frame in range(frames):
        standard = (clip_ref[frame].reshape(-1, width).astype(f32) - mean) * inv
        shortcut = back_dot(cot_ref[frame].reshape(-1, out_width), short_ref[...])
        grad = grad_ref[frame]
        at = frame - (frames - lead)
        if at >= 0:
            following = after_ref[at * places : (at + 1) * places].astype(f32) * slope_ref[at]
            grad = grad + jnp.where(is_last, 0.0, following)
        grad = (grad - mean_grad - standard * mean_cross) * inv + shortcut
        out_ref[frame] = grad.astype(bf16).reshape(rows, cols, width)


def first_kernel(total_ref, got_ref, keep_ref, *send_refs):
    at = lax.axis_index("dp")
    z, x, core = at // 4, lax.rem(at // 2, 2), lax.rem(at, 2)
    y = lax.axis_index("ctx")
    plane = x + 2 * y
    for step, target in enumerate((keep_ref, *send_refs)):
        for inner in range(4):
            to_plane = jnp.where(core == 0, lax.bitwise_xor(plane, step), inner)
            to_z = jnp.where(core == 0, inner, lax.bitwise_xor(z, step))
            to_x, to_y = lax.rem(to_plane, 2), to_plane // 2
            value = total_ref[to_y, to_z, to_x, core] + got_ref[to_y, to_z, to_x].astype(f32)
            target[inner] = value.astype(target.dtype)


def second_kernel(keep_ref, a_ref, b_ref, c_ref, own_ref, *send_refs):
    at = lax.axis_index("dp")
    plane = lax.rem(at // 2, 2) + 2 * lax.axis_index("ctx")
    here = jnp.where(lax.rem(at, 2) == 0, at // 4, plane)
    for step, target in enumerate((own_ref, *send_refs)):
        to = lax.bitwise_xor(here, step)
        value = keep_ref[to] + a_ref[to].astype(f32) + (b_ref[to].astype(f32) + c_ref[to].astype(f32))
        target[...] = value.astype(target.dtype)


def last_kernel(scale, own_ref, a_ref, b_ref, c_ref, conv_ref, short_ref):
    value = own_ref[...] + a_ref[...].astype(f32) + (b_ref[...].astype(f32) + c_ref[...].astype(f32))
    value = value * scale
    conv_ref[...] = value[: conv_ref.shape[0]]
    short_ref[...] = value[conv_ref.shape[0] :]


def from_behind(value, axis, steps):
    count = lax.axis_size(axis)
    initial, last = (max(0, -steps), min(count, count - steps))
    return lax.ppermute(value, axis, [(source, source + steps) for source in range(initial, last)])


def others_total(value):
    count = lax.axis_size("ctx")
    total = None
    for step in range(1, count):
        got = lax.ppermute(value, "ctx", [(source, (source + step) % count) for source in range(count)])
        total = got if total is None else total + got
    return jnp.zeros_like(value) if total is None else total


def swap(value, core_0, core_1):
    dp, ctx = lax.axis_size("dp"), lax.axis_size("ctx")
    masks = (core_0, core_1)
    pairs = []
    for source in range(dp * ctx):
        at, side = divmod(source, ctx)
        dp_mask, ctx_mask = masks[at % 2]
        pairs.append((source, (at ^ dp_mask) * ctx + (side ^ ctx_mask)))
    return lax.ppermute(value, ("dp", "ctx"), pairs)


def exchange(sends, plane_core):
    got = []
    for step in (3, 2, 1):
        masks = [None, None]
        masks[plane_core] = (2 * (step % 2), step // 2)
        masks[1 - plane_core] = (4 * step, 0)
        got.append(swap(sends[step - 1], *masks))
    return got


def sort_first(total, got):
    halves, blocks, rows, cols = got.shape
    part = (4, rows, cols)
    return call(
        first_kernel,
        [jax.ShapeDtypeStruct(part, f32)] + [jax.ShapeDtypeStruct(part, bf16)] * 3,
    )(total.reshape(halves, blocks // 2, 2, 2, rows, cols), got.reshape(halves, blocks // 2, 2, rows, cols))


def sort_second(keep, *got):
    part = keep.shape[1:]
    return call(
        second_kernel,
        [jax.ShapeDtypeStruct(part, f32)] + [jax.ShapeDtypeStruct(part, bf16)] * 3,
    )(keep, *got)


def add_last(mine, from_a, from_b, from_c, conv_rows, short_rows, scale):
    cols = mine.shape[1]
    return call(
        functools.partial(last_kernel, scale),
        [jax.ShapeDtypeStruct((conv_rows, cols), f32), jax.ShapeDtypeStruct((short_rows, cols), f32)],
        moved=mine.size * 12,
    )(mine, from_a, from_b, from_c)


def body(clip_in, norm_gain, norm_bias, conv_weight, short_weight, out_cotangent):
    batch_clips, frames, height, breadth, in_width = clip_in.shape
    assert batch_clips == 1
    out_width = conv_weight.shape[1]
    per_group = in_width // GROUPS
    dp_size, ctx_size = lax.axis_size("dp"), lax.axis_size("ctx")
    total_frames = frames * ctx_size
    members = total_frames * height * breadth * per_group
    scale = 1.0 / (batch_clips * dp_size * total_frames)
    places = frames * height * breadth
    clip = clip_in[0]
    cot = out_cotangent[0]
    gain = norm_gain.reshape(1, in_width)
    bias = norm_bias.reshape(1, in_width)
    conv_all = TAPS * in_width
    work = places * conv_all * out_width * 2

    lead = KT - 1
    stats, last_clip = call(
        start_kernel,
        [jax.ShapeDtypeStruct((8, in_width), f32), jax.ShapeDtypeStruct((lead,) + clip.shape[1:], bf16)],
        flops=work, moved=clip.size * 2,
    )(clip)
    other = others_total(stats)
    halo = from_behind(last_clip, "ctx", 1)

    half_cot = pltpu.VMEM((KS, 2, height + 2, breadth, out_width), bf16)
    first_part, leading, cot_t = call(
        back_first_kernel,
        [
            jax.ShapeDtypeStruct((2, height * breadth, in_width), f32),
            jax.ShapeDtypeStruct((lead, height * breadth, in_width), bf16),
            jax.ShapeDtypeStruct((out_width, places), bf16),
        ],
        [half_cot],
        flops=work, moved=conv_weight.size * 2,
    )(cot, conv_weight)
    padded = (KS, frames, height + 2, breadth, in_width)
    late_at = (KT - 1) * KS * KS * in_width
    hidden, early, late = call(
        functools.partial(weight_own_kernel, members),
        [
            jax.ShapeDtypeStruct(padded, bf16),
            jax.ShapeDtypeStruct((out_width, late_at), f32),
            jax.ShapeDtypeStruct((conv_all + in_width - late_at, out_width), f32),
        ],
        flops=work, moved=cot.size * 2,
    )(clip, stats, other, gain, bias, cot_t)

    staged = dp_size == 16 and ctx_size == 2
    conv_rows, short_rows = conv_all // dp_size, in_width // dp_size
    if staged:
        cols = out_width // ctx_size
        block = (conv_rows + short_rows, cols)
        outs = [
            jax.ShapeDtypeStruct((ctx_size, dp_size) + block, f32),
            jax.ShapeDtypeStruct((ctx_size, dp_size // 2) + block, bf16),
        ]
        split = (conv_rows, short_rows, conv_all)
    else:
        outs = [jax.ShapeDtypeStruct((conv_all + in_width, out_width), f32)]
        split = None
    hidden_lead, *parts = call(
        functools.partial(weight_halo_kernel, members, split),
        [jax.ShapeDtypeStruct((KS, lead) + padded[2:], bf16)] + outs,
        flops=work // 3, moved=cot.size * 2,
    )(halo, clip, stats, other, gain, bias, cot_t, early, late)

    first_part, hidden_lead = lax.optimization_barrier((first_part, hidden_lead))
    back_part = call(
        back_second_kernel,
        jax.ShapeDtypeStruct((frames, height * breadth, in_width), f32),
        [half_cot],
        flops=work // 4,
    )(cot, conv_weight, first_part)
    if staged:
        got, back_part = lax.optimization_barrier((swap(parts[1], (1, 0), (1, 0)), back_part))
        keep, *sends = sort_first(parts[0], got)
        got = exchange(sends, 0)
        hidden, keep = lax.optimization_barrier((hidden, keep))
    forward = call(
        forward_kernel,
        jax.ShapeDtypeStruct((frames, height, breadth, out_width), bf16),
        flops=work // 4,
    )(hidden_lead, hidden, clip, conv_weight, short_weight)
    anywhere, vmem = pl.BlockSpec(memory_space=pl.ANY), pl.BlockSpec(memory_space=pltpu.VMEM)
    grad, slope, sums, parcel, clip_out = call(
        functools.partial(activation_kernel, members),
        [
            jax.ShapeDtypeStruct((frames, height * breadth, in_width), f32),
            jax.ShapeDtypeStruct((lead, height * breadth, in_width), f32),
            jax.ShapeDtypeStruct((8, in_width), f32),
            jax.ShapeDtypeStruct((lead * height * breadth + 16, in_width), bf16),
            jax.ShapeDtypeStruct(forward.shape, bf16),
        ],
        [pltpu.SemaphoreType.DMA],
        in_specs=[vmem] * 9,
        out_specs=[vmem] * 4 + [anywhere],
    )(back_part, leading, clip, halo, stats, other, gain, bias, forward)
    if ctx_size == 2:
        after = lax.ppermute(parcel, "ctx", [(0, 1), (1, 0)])
    else:
        after = from_behind(leading, "ctx", -1).reshape(-1, in_width)
        after = jnp.concatenate([after, pieces_block(others_total(sums))], axis=0)
    if staged:
        *got, sums = lax.optimization_barrier((*got, sums))
        mine, *sends = sort_second(keep, *got)
        got = exchange(sends, 1)
        conv_grad, short_grad = add_last(mine, *got, conv_rows, short_rows, scale)
        after, mine = lax.optimization_barrier((after, mine))
    else:
        summed = []
        for part in (parts[0][:conv_all], parts[0][conv_all:]):
            part = lax.psum_scatter(part, "dp", scatter_dimension=0, tiled=True)
            part = lax.psum_scatter(part, "ctx", scatter_dimension=1, tiled=True)
            summed.append(part * scale)
        conv_grad, short_grad = summed
    clip_grad = call(
        functools.partial(finish_kernel, members),
        jax.ShapeDtypeStruct((frames, height, breadth, in_width), bf16),
        flops=work // 20, moved=cot.size * 4,
    )(grad, slope, sums, after, clip, stats, other, cot, short_weight)
    return (clip_out[None], clip_grad[None], conv_grad, short_grad)


def solution(mesh):
    return jax.shard_map(
        body,
        mesh=mesh,
        in_specs=(
            P("dp", "ctx", None, None, None),
            P(),
            P(),
            P(),
            P(),
            P("dp", "ctx", None, None, None),
        ),
        out_specs=(
            P("dp", "ctx", None, None, None),
            P("dp", "ctx", None, None, None),
            P("dp", "ctx"),
            P("dp", "ctx"),
        ),
        check_vma=False,
    )
```

```python
import functools

import jax
import jax.numpy as jnp
from jax import lax
from jax.experimental import pallas as pl
from jax.experimental.pallas import tpu as pltpu
from jax.sharding import PartitionSpec as P

GROUPS = 32
KT = 3
KS = 3
TAPS = KT * KS * KS
VMEM_BYTES = 28 * 1024 * 1024

epsilon = 1e-06
f32 = jnp.float32
bf16 = jnp.bfloat16


def call(kernel, outs, scratch=(), flops=0, moved=0, in_specs=None, out_specs=None):
    specs = {} if in_specs is None else {"in_specs": in_specs}
    if out_specs is not None:
        specs["out_specs"] = out_specs
    return pl.pallas_call(
        kernel,
        out_shape=outs,
        **specs,
        scratch_shapes=list(scratch),
        compiler_params=pltpu.CompilerParams(vmem_limit_bytes=VMEM_BYTES),
        cost_estimate=pl.CostEstimate(flops=flops, bytes_accessed=moved, transcendentals=0),
    )


def group_totals(rows):
    width = rows.shape[1]
    per_group = width // GROUPS
    row = lax.broadcasted_iota(jnp.int32, (width, width), 0) // per_group
    col = lax.broadcasted_iota(jnp.int32, (width, width), 1) // per_group
    same = (row == col).astype(f32)
    return lax.dot_general(
        rows, same, (((1,), (0,)), ((), ())), precision=lax.Precision.HIGHEST, preferred_element_type=f32
    )


def two_rows(first, second):
    at = lax.broadcasted_iota(jnp.int32, (8, first.shape[1]), 0)
    return jnp.where(at == 0, first, jnp.where(at == 1, second, 0.0))


def column_totals(value):
    return jnp.sum(value, axis=0, keepdims=True)


def in_pieces(value):
    high = value.astype(bf16)
    rest = value - high.astype(f32)
    middle = rest.astype(bf16)
    low = (rest - middle.astype(f32)).astype(bf16)
    return high, middle, low


def pieces_block(totals):
    pieces = [piece[0:2].astype(f32) for piece in in_pieces(totals)]
    zero = jnp.zeros((10, totals.shape[1]), f32)
    return jnp.concatenate(pieces + [zero], axis=0).astype(bf16)


def start_kernel(clip_ref, stats_ref, last_ref):
    frames = clip_ref.shape[0]
    width = clip_ref.shape[-1]
    total = jnp.zeros((1, width), f32)
    square = jnp.zeros((1, width), f32)
    for frame in range(frames):
        value = clip_ref[frame].reshape(-1, width).astype(f32)
        total = total + column_totals(value)
        square = square + column_totals(value * value)
    stats_ref[...] = group_totals(two_rows(total, square))
    last_ref[...] = clip_ref[frames - last_ref.shape[0] :]


def whole(parcel):
    pieces = parcel[parcel.shape[0] - 16 :].astype(f32)
    return pieces[0:2] + (pieces[2:4] + pieces[4:6])


def moments(stats, other, members):
    totals = stats[0:2] + other[0:2]
    mean = totals[0:1] / members
    variance = totals[1:2] / members - mean * mean
    return mean, lax.rsqrt(variance + epsilon)


def shift_columns(value, step):
    rows, cols, width = value.shape
    flat = value.reshape(rows * cols, width)
    rolled = pltpu.roll(flat, (-step) % (rows * cols), 0).reshape(rows, cols, width)
    at = lax.broadcasted_iota(jnp.int32, (rows, cols, width), 1)
    edge = cols - 1 if step == 1 else 0
    return jnp.where(at == edge, 0.0, rolled)


def place(padded, frame, value):
    rows, cols, width = value.shape
    for j, step in enumerate((-1, 0, 1)):
        moved = value if step == 0 else shift_columns(value, step)
        padded[j, frame, 1 : rows + 1] = moved.astype(bf16)


def clear_edges(padded):
    rows = padded.shape[2]
    zero = jnp.zeros(padded.shape[:2] + padded.shape[3:], bf16)
    padded[:, :, 0] = zero
    padded[:, :, rows - 1] = zero


def hidden_of(value, mean, inv, gain, bias):
    affine = (value.astype(f32) - mean) * inv * gain + bias
    return affine * jax.nn.sigmoid(affine)


def tap_block(padded, frames, rows, t, i):
    width = padded.shape[-1]
    return [padded[j, t : t + frames, i : i + rows].reshape(-1, width) for j in range(KS)]


def groups_of_taps():
    return ((0, 1), (2,))


def weight_own_kernel(
    members,
    clip_ref, stats_ref, other_ref, gain_ref, bias_ref, cot_t_ref,
    padded, early_ref, late_ref,
):
    frames, rows, cols, width = clip_ref.shape
    mean, inv = moments(stats_ref, other_ref, members)
    clear_edges(padded)
    for frame in range(frames):
        place(padded, frame, hidden_of(clip_ref[frame], mean, inv, gain_ref[...], bias_ref[...]))
    per_frame = rows * cols
    for t in range(KT - 1, -1, -1):
        skipped = KT - 1 - t
        cot_t = cot_t_ref[:, skipped * per_frame :]
        base = row = t * KS * KS * width
        for group in groups_of_taps():
            parts = []
            for i in group:
                parts += tap_block(padded, frames - skipped, rows, 0, i)
            if t == KT - 1 and group[-1] == KS - 1:
                parts.append(clip_ref[...].reshape(-1, width))
            part = jnp.dot(cot_t, jnp.concatenate(parts, axis=1), preferred_element_type=f32)
            stop = row + part.shape[1]
            if t == KT - 1:
                late_ref[row - base : stop - base, :] = part.T
            else:
                early_ref[:, row:stop] = part
            row = stop


def weight_halo_kernel(
    members, split,
    halo_ref, clip_ref, stats_ref, other_ref, gain_ref, bias_ref, cot_t_ref, early_ref, late_ref,
    padded, total, *rest,
):
    at_start = lax.axis_index("ctx") == 0
    lead, rows, cols, width = halo_ref.shape
    mean, inv = moments(stats_ref, other_ref, members)
    clear_edges(padded)
    for frame in range(lead):
        value = jnp.where(at_start, clip_ref[0].astype(f32), halo_ref[frame].astype(f32))
        place(padded, frame, hidden_of(value, mean, inv, gain_ref[...], bias_ref[...]))
    per_frame = rows * cols

    def give(part, begin):
        if split is None:
            total[begin : begin + part.shape[0], :] = part
        else:
            scatter_rows(total, part, begin, split)

    give(late_ref[...], early_ref.shape[1])
    row = 0
    for t in range(KT - 1):
        count = lead - t
        for group in groups_of_taps():
            parts = []
            for i in group:
                parts += tap_block(padded, count, rows, t, i)
            part = jnp.dot(
                cot_t_ref[:, : count * per_frame], jnp.concatenate(parts, axis=1), preferred_element_type=f32
            )
            stop = row + part.shape[1]
            give((part + early_ref[:, row:stop]).T, row)
            row = stop
    if split is not None:
        (send_ref,) = rest
        core = lax.rem(lax.axis_index("dp"), 2)
        halves, blocks = send_ref.shape[:2]
        for half in range(halves):
            for k in range(blocks):
                send_ref[half, k] = total[half, 2 * k + 1 - core].astype(bf16)


def scatter_rows(total, part, begin, split):
    conv_rows, short_rows, conv_all = split
    halves = total.shape[0]
    row, stop = begin, begin + part.shape[0]
    width = total.shape[-1]
    while row < stop:
        if row < conv_all:
            block, offset = divmod(row, conv_rows)
            count = min(conv_rows - offset, stop - row, conv_all - row)
            target = offset
        else:
            block, offset = divmod(row - conv_all, short_rows)
            count = min(short_rows - offset, stop - row)
            target = conv_rows + offset
        for half in range(halves):
            total[half, block, target : target + count, :] = part[
                row - begin : row - begin + count, half * width : (half + 1) * width
            ]
        row += count


def forward_kernel(padded_lead, padded, clip_ref, weight_ref, short_ref, out_ref):
    frames, rows, cols, width = clip_ref.shape
    lead = padded_lead.shape[1]
    for frame in range(frames):
        parts = []
        for t in range(KT):
            source, at = (padded_lead, frame + t) if frame + t < lead else (padded, frame + t - lead)
            for i in range(KS):
                parts += tap_block(source, 1, rows, at, i)
        result = jnp.dot(jnp.concatenate(parts, axis=1), weight_ref[...], preferred_element_type=f32)
        result = result + jnp.dot(
            clip_ref[frame].reshape(-1, width), short_ref[...], preferred_element_type=f32
        )
        out_ref[frame] = result.astype(bf16).reshape(rows, cols, -1)


def back_weights(weight_ref, width, taps_t):
    bands = []
    for t in taps_t:
        bands.append(
            jnp.concatenate(
                [weight_ref[(t * KS * KS + q) * width : (t * KS * KS + q + 1) * width, :] for q in range(KS * KS)],
                axis=1,
            )
        )
    return jnp.concatenate(bands, axis=0) if len(bands) > 1 else bands[0]


def spatial_block(padded, frame, rows):
    out_width = padded.shape[-1]
    parts = []
    for i in range(KS):
        for j in range(KS):
            parts.append(padded[2 - j, frame, 2 - i : 2 - i + rows].reshape(-1, out_width))
    return jnp.concatenate(parts, axis=1)


def back_dot(block, weights):
    return lax.dot_general(block, weights, (((1,), (1,)), ((), ())), preferred_element_type=f32)


def back_products(begin, count, cot_ref, weight_ref, width, padded):
    rows, cols, out_width = cot_ref.shape[1:]
    clear_edges(padded)
    late = back_weights(weight_ref, width, (2, 1))
    early = back_weights(weight_ref, width, (0,))
    products = []
    for at in range(count):
        place(padded, at, cot_ref[begin + at].astype(f32))
        block = spatial_block(padded, at, rows)
        both = back_dot(block, late)
        products.append((both[:, :width], both[:, width:], back_dot(block, early)))
    return products


def back_first_kernel(cot_ref, weight_ref, out_ref, before_ref, cot_t_ref, padded):
    out_width = cot_ref.shape[-1]
    at_start = lax.axis_index("ctx") == 0
    cot_t_ref[...] = cot_ref[...].reshape(-1, out_width).T
    width = out_ref.shape[-1]
    (a2, a1, a0), (b2, b1, b0) = back_products(0, 2, cot_ref, weight_ref, width, padded)
    last = a1 + b0
    before_ref[0] = a0.astype(bf16)
    before_ref[1] = last.astype(bf16)
    out_ref[0] = a2 + b1 + jnp.where(at_start, a0 + last, 0.0)
    out_ref[1] = b2


def slope_of(value, mean, inv, gain, bias):
    standard = (value.astype(f32) - mean) * inv
    affine = standard * gain + bias
    logistic = jax.nn.sigmoid(affine)
    return standard, logistic * (1.0 + affine * (1.0 - logistic)) * gain


def back_second_kernel(
    members,
    cot_ref, weight_ref, first_ref, leading_ref, halo_ref, stats_ref, other_ref, gain_ref, bias_ref,
    out_ref, share_ref, padded,
):
    mean, inv = moments(stats_ref, other_ref, members)
    total = jnp.zeros((1, out_ref.shape[-1]), f32)
    cross = total
    for frame in range(leading_ref.shape[0]):
        value = halo_ref[frame].reshape(-1, out_ref.shape[-1])
        standard, slope = slope_of(value, mean, inv, gain_ref[...], bias_ref[...])
        grad = leading_ref[frame].astype(f32) * slope
        total = total + column_totals(grad)
        cross = cross + column_totals(grad * standard)
    at_start = lax.axis_index("ctx") == 0
    share_ref[...] = jnp.where(at_start, 0.0, two_rows(total, cross))
    width = out_ref.shape[-1]
    frames = cot_ref.shape[0]
    out_ref[0:2] = first_ref[...]
    for frame, (same, one, two) in enumerate(back_products(2, frames - 2, cot_ref, weight_ref, width, padded), 2):
        out_ref[frame] = same
        out_ref[frame - 1] += one
        out_ref[frame - 2] += two


def activation_kernel(
    members,
    part_ref, share_ref, leading_ref, clip_ref, stats_ref, other_ref, gain_ref, bias_ref, forward_ref,
    grad_ref, slope_ref, sums_ref, out_ref, whole_ref, sem,
):
    copy = pltpu.make_async_copy(forward_ref, whole_ref, sem)
    copy.start()
    frames, rows, cols, width = clip_ref.shape
    places = rows * cols
    gain = gain_ref[...]
    mean, inv = moments(stats_ref, other_ref, members)

    total = share_ref[0:1]
    cross = share_ref[1:2]
    lead = leading_ref.shape[0]
    for frame in range(lead):
        out_ref[frame * places : (frame + 1) * places] = leading_ref[frame]
    for frame in range(frames):
        standard, slope = slope_of(clip_ref[frame].reshape(-1, width), mean, inv, gain, bias_ref[...])
        grad = part_ref[frame] * slope
        grad_ref[frame] = grad
        if frame >= frames - lead:
            slope_ref[frame - (frames - lead)] = slope
        total = total + column_totals(grad)
        cross = cross + column_totals(grad * standard)
    sums = group_totals(two_rows(total, cross))
    sums_ref[...] = sums
    out_ref[lead * places :] = pieces_block(sums)
    copy.wait()


def finish_kernel(
    members,
    grad_ref, slope_ref, sums_ref, after_ref, clip_ref, stats_ref, other_ref, cot_ref, short_ref,
    out_ref,
):
    frames, rows, cols, width = clip_ref.shape
    places = rows * cols
    out_width = cot_ref.shape[-1]
    lead = slope_ref.shape[0]
    is_last = lax.axis_index("ctx") == lax.axis_size("ctx") - 1
    mean, inv = moments(stats_ref, other_ref, members)
    sums = sums_ref[0:2] + whole(after_ref)
    mean_grad = sums[0:1] / members
    mean_cross = sums[1:2] / members
    for frame in range(frames):
        standard = (clip_ref[frame].reshape(-1, width).astype(f32) - mean) * inv
        shortcut = back_dot(cot_ref[frame].reshape(-1, out_width), short_ref[...])
        grad = grad_ref[frame]
        at = frame - (frames - lead)
        if at >= 0:
            following = after_ref[at * places : (at + 1) * places].astype(f32) * slope_ref[at]
            grad = grad + jnp.where(is_last, 0.0, following)
        grad = (grad - mean_grad - standard * mean_cross) * inv + shortcut
        out_ref[frame] = grad.astype(bf16).reshape(rows, cols, width)


def first_kernel(total_ref, got_ref, keep_ref, *send_refs):
    at = lax.axis_index("dp")
    z, x, core = at // 4, lax.rem(at // 2, 2), lax.rem(at, 2)
    y = lax.axis_index("ctx")
    plane = x + 2 * y
    for step, target in enumerate((keep_ref, *send_refs)):
        for inner in range(4):
            to_plane = jnp.where(core == 0, lax.bitwise_xor(plane, step), inner)
            to_z = jnp.where(core == 0, inner, lax.bitwise_xor(z, step))
            to_x, to_y = lax.rem(to_plane, 2), to_plane // 2
            value = total_ref[to_y, to_z, to_x, core] + got_ref[to_y, to_z, to_x].astype(f32)
            target[inner] = value.astype(target.dtype)


def second_kernel(keep_ref, a_ref, b_ref, c_ref, own_ref, *send_refs):
    at = lax.axis_index("dp")
    plane = lax.rem(at // 2, 2) + 2 * lax.axis_index("ctx")
    here = jnp.where(lax.rem(at, 2) == 0, at // 4, plane)
    for step, target in enumerate((own_ref, *send_refs)):
        to = lax.bitwise_xor(here, step)
        value = keep_ref[to] + a_ref[to].astype(f32) + (b_ref[to].astype(f32) + c_ref[to].astype(f32))
        target[...] = value.astype(target.dtype)


def last_kernel(scale, own_ref, a_ref, b_ref, c_ref, conv_ref, short_ref):
    value = own_ref[...] + a_ref[...].astype(f32) + (b_ref[...].astype(f32) + c_ref[...].astype(f32))
    value = value * scale
    conv_ref[...] = value[: conv_ref.shape[0]]
    short_ref[...] = value[conv_ref.shape[0] :]


def from_behind(value, axis, steps):
    count = lax.axis_size(axis)
    initial, last = (max(0, -steps), min(count, count - steps))
    return lax.ppermute(value, axis, [(source, source + steps) for source in range(initial, last)])


def others_total(value):
    count = lax.axis_size("ctx")
    total = None
    for step in range(1, count):
        got = lax.ppermute(value, "ctx", [(source, (source + step) % count) for source in range(count)])
        total = got if total is None else total + got
    return jnp.zeros_like(value) if total is None else total


def swap(value, core_0, core_1):
    dp, ctx = lax.axis_size("dp"), lax.axis_size("ctx")
    masks = (core_0, core_1)
    pairs = []
    for source in range(dp * ctx):
        at, side = divmod(source, ctx)
        dp_mask, ctx_mask = masks[at % 2]
        pairs.append((source, (at ^ dp_mask) * ctx + (side ^ ctx_mask)))
    return lax.ppermute(value, ("dp", "ctx"), pairs)


def exchange(sends, plane_core):
    got = []
    for step in (3, 2, 1):
        masks = [None, None]
        masks[plane_core] = (2 * (step % 2), step // 2)
        masks[1 - plane_core] = (4 * step, 0)
        got.append(swap(sends[step - 1], *masks))
    return got


def sort_first(total, got):
    halves, blocks, rows, cols = got.shape
    part = (4, rows, cols)
    return call(
        first_kernel,
        [jax.ShapeDtypeStruct(part, f32)] + [jax.ShapeDtypeStruct(part, bf16)] * 3,
    )(total.reshape(halves, blocks // 2, 2, 2, rows, cols), got.reshape(halves, blocks // 2, 2, rows, cols))


def sort_second(keep, *got):
    part = keep.shape[1:]
    return call(
        second_kernel,
        [jax.ShapeDtypeStruct(part, f32)] + [jax.ShapeDtypeStruct(part, bf16)] * 3,
    )(keep, *got)


def add_last(mine, from_a, from_b, from_c, conv_rows, short_rows, scale):
    cols = mine.shape[1]
    return call(
        functools.partial(last_kernel, scale),
        [jax.ShapeDtypeStruct((conv_rows, cols), f32), jax.ShapeDtypeStruct((short_rows, cols), f32)],
        moved=mine.size * 12,
    )(mine, from_a, from_b, from_c)


def body(clip_in, norm_gain, norm_bias, conv_weight, short_weight, out_cotangent):
    batch_clips, frames, height, breadth, in_width = clip_in.shape
    assert batch_clips == 1
    out_width = conv_weight.shape[1]
    per_group = in_width // GROUPS
    dp_size, ctx_size = lax.axis_size("dp"), lax.axis_size("ctx")
    total_frames = frames * ctx_size
    members = total_frames * height * breadth * per_group
    scale = 1.0 / (batch_clips * dp_size * total_frames)
    places = frames * height * breadth
    clip = clip_in[0]
    cot = out_cotangent[0]
    gain = norm_gain.reshape(1, in_width)
    bias = norm_bias.reshape(1, in_width)
    conv_all = TAPS * in_width
    work = places * conv_all * out_width * 2

    lead = KT - 1
    stats, last_clip = call(
        start_kernel,
        [jax.ShapeDtypeStruct((8, in_width), f32), jax.ShapeDtypeStruct((lead,) + clip.shape[1:], bf16)],
        flops=work, moved=clip.size * 2,
    )(clip)
    other = others_total(stats)
    halo = from_behind(last_clip, "ctx", 1)

    half_cot = pltpu.VMEM((KS, 2, height + 2, breadth, out_width), bf16)
    first_part, leading, cot_t = call(
        back_first_kernel,
        [
            jax.ShapeDtypeStruct((2, height * breadth, in_width), f32),
            jax.ShapeDtypeStruct((lead, height * breadth, in_width), bf16),
            jax.ShapeDtypeStruct((out_width, places), bf16),
        ],
        [half_cot],
        flops=work, moved=conv_weight.size * 2,
    )(cot, conv_weight)
    padded = (KS, frames, height + 2, breadth, in_width)
    late_at = (KT - 1) * KS * KS * in_width
    hidden, early, late = call(
        functools.partial(weight_own_kernel, members),
        [
            jax.ShapeDtypeStruct(padded, bf16),
            jax.ShapeDtypeStruct((out_width, late_at), f32),
            jax.ShapeDtypeStruct((conv_all + in_width - late_at, out_width), f32),
        ],
        flops=work, moved=cot.size * 2,
    )(clip, stats, other, gain, bias, cot_t)

    staged = dp_size == 16 and ctx_size == 2
    conv_rows, short_rows = conv_all // dp_size, in_width // dp_size
    if staged:
        cols = out_width // ctx_size
        block = (conv_rows + short_rows, cols)
        outs = [
            jax.ShapeDtypeStruct((ctx_size, dp_size) + block, f32),
            jax.ShapeDtypeStruct((ctx_size, dp_size // 2) + block, bf16),
        ]
        split = (conv_rows, short_rows, conv_all)
    else:
        outs = [jax.ShapeDtypeStruct((conv_all + in_width, out_width), f32)]
        split = None
    hidden_lead, *parts = call(
        functools.partial(weight_halo_kernel, members, split),
        [jax.ShapeDtypeStruct((KS, lead) + padded[2:], bf16)] + outs,
        flops=work // 3, moved=cot.size * 2,
    )(halo, clip, stats, other, gain, bias, cot_t, early, late)

    first_part, hidden_lead = lax.optimization_barrier((first_part, hidden_lead))
    back_part, share = call(
        functools.partial(back_second_kernel, members),
        [
            jax.ShapeDtypeStruct((frames, height * breadth, in_width), f32),
            jax.ShapeDtypeStruct((8, in_width), f32),
        ],
        [half_cot],
        flops=work // 4,
    )(cot, conv_weight, first_part, leading, halo, stats, other, gain, bias)
    if staged:
        got, back_part = lax.optimization_barrier((swap(parts[1], (1, 0), (1, 0)), back_part))
        keep, *sends = sort_first(parts[0], got)
        got = exchange(sends, 0)
        hidden, keep = lax.optimization_barrier((hidden, keep))
    forward = call(
        forward_kernel,
        jax.ShapeDtypeStruct((frames, height, breadth, out_width), bf16),
        flops=work // 4,
    )(hidden_lead, hidden, clip, conv_weight, short_weight)
    anywhere, vmem = pl.BlockSpec(memory_space=pl.ANY), pl.BlockSpec(memory_space=pltpu.VMEM)
    grad, slope, sums, parcel, clip_out = call(
        functools.partial(activation_kernel, members),
        [
            jax.ShapeDtypeStruct((frames, height * breadth, in_width), f32),
            jax.ShapeDtypeStruct((lead, height * breadth, in_width), f32),
            jax.ShapeDtypeStruct((8, in_width), f32),
            jax.ShapeDtypeStruct((lead * height * breadth + 16, in_width), bf16),
            jax.ShapeDtypeStruct(forward.shape, bf16),
        ],
        [pltpu.SemaphoreType.DMA],
        in_specs=[vmem] * 9,
        out_specs=[vmem] * 4 + [anywhere],
    )(back_part, share, leading, clip, stats, other, gain, bias, forward)
    if ctx_size == 2:
        after = lax.ppermute(parcel, "ctx", [(0, 1), (1, 0)])
    else:
        after = from_behind(leading, "ctx", -1).reshape(-1, in_width)
        after = jnp.concatenate([after, pieces_block(others_total(sums))], axis=0)
    if staged:
        *got, sums = lax.optimization_barrier((*got, sums))
        mine, *sends = sort_second(keep, *got)
        got = exchange(sends, 1)
        conv_grad, short_grad = add_last(mine, *got, conv_rows, short_rows, scale)
        after, mine = lax.optimization_barrier((after, mine))
    else:
        summed = []
        for part in (parts[0][:conv_all], parts[0][conv_all:]):
            part = lax.psum_scatter(part, "dp", scatter_dimension=0, tiled=True)
            part = lax.psum_scatter(part, "ctx", scatter_dimension=1, tiled=True)
            summed.append(part * scale)
        conv_grad, short_grad = summed
    clip_grad = call(
        functools.partial(finish_kernel, members),
        jax.ShapeDtypeStruct((frames, height, breadth, in_width), bf16),
        flops=work // 20, moved=cot.size * 4,
    )(grad, slope, sums, after, clip, stats, other, cot, short_weight)
    return (clip_out[None], clip_grad[None], conv_grad, short_grad)


def solution(mesh):
    return jax.shard_map(
        body,
        mesh=mesh,
        in_specs=(
            P("dp", "ctx", None, None, None),
            P(),
            P(),
            P(),
            P(),
            P("dp", "ctx", None, None, None),
        ),
        out_specs=(
            P("dp", "ctx", None, None, None),
            P("dp", "ctx", None, None, None),
            P("dp", "ctx"),
            P("dp", "ctx"),
        ),
        check_vma=False,
    )
```

```python
import functools

import jax
import jax.numpy as jnp
from jax import lax
from jax.experimental import pallas as pl
from jax.experimental.pallas import tpu as pltpu
from jax.sharding import PartitionSpec as P

GROUPS = 32
KT = 3
KS = 3
TAPS = KT * KS * KS
VMEM_BYTES = 28 * 1024 * 1024

epsilon = 1e-06
f32 = jnp.float32
bf16 = jnp.bfloat16


def call(kernel, outs, scratch=(), flops=0, moved=0, in_specs=None, out_specs=None):
    specs = {} if in_specs is None else {"in_specs": in_specs}
    if out_specs is not None:
        specs["out_specs"] = out_specs
    return pl.pallas_call(
        kernel,
        out_shape=outs,
        **specs,
        scratch_shapes=list(scratch),
        compiler_params=pltpu.CompilerParams(vmem_limit_bytes=VMEM_BYTES),
        cost_estimate=pl.CostEstimate(flops=flops, bytes_accessed=moved, transcendentals=0),
    )


def group_totals(rows):
    width = rows.shape[1]
    per_group = width // GROUPS
    row = lax.broadcasted_iota(jnp.int32, (width, width), 0) // per_group
    col = lax.broadcasted_iota(jnp.int32, (width, width), 1) // per_group
    same = (row == col).astype(bf16)
    stacked = jnp.concatenate([piece.astype(f32) for piece in in_pieces(rows)], axis=0).astype(bf16)
    totals = jnp.dot(stacked, same, preferred_element_type=f32)
    return totals[0:8] + (totals[8:16] + totals[16:24])


def two_rows(first, second):
    at = lax.broadcasted_iota(jnp.int32, (8, first.shape[1]), 0)
    return jnp.where(at == 0, first, jnp.where(at == 1, second, 0.0))


def column_totals(value):
    return jnp.sum(value, axis=0, keepdims=True)


def in_pieces(value):
    high = value.astype(bf16)
    rest = value - high.astype(f32)
    middle = rest.astype(bf16)
    low = (rest - middle.astype(f32)).astype(bf16)
    return high, middle, low


def pieces_block(totals):
    pieces = [piece[0:2].astype(f32) for piece in in_pieces(totals)]
    zero = jnp.zeros((10, totals.shape[1]), f32)
    return jnp.concatenate(pieces + [zero], axis=0).astype(bf16)


def start_kernel(clip_ref, stats_ref, last_ref):
    frames = clip_ref.shape[0]
    width = clip_ref.shape[-1]
    total = jnp.zeros((1, width), f32)
    square = jnp.zeros((1, width), f32)
    for frame in range(frames):
        value = clip_ref[frame].reshape(-1, width).astype(f32)
        total = total + column_totals(value)
        square = square + column_totals(value * value)
    stats_ref[...] = group_totals(two_rows(total, square))
    last_ref[...] = clip_ref[frames - last_ref.shape[0] :]


def whole(parcel):
    pieces = parcel[parcel.shape[0] - 16 :].astype(f32)
    return pieces[0:2] + (pieces[2:4] + pieces[4:6])


def moments(stats, other, members):
    totals = stats[0:2] + other[0:2]
    mean = totals[0:1] / members
    variance = totals[1:2] / members - mean * mean
    return mean, lax.rsqrt(variance + epsilon)


def shift_columns(value, step):
    rows, cols, width = value.shape
    flat = value.reshape(rows * cols, width)
    rolled = pltpu.roll(flat, (-step) % (rows * cols), 0).reshape(rows, cols, width)
    at = lax.broadcasted_iota(jnp.int32, (rows, cols, width), 1)
    edge = cols - 1 if step == 1 else 0
    return jnp.where(at == edge, 0.0, rolled)


def place(padded, frame, value):
    rows, cols, width = value.shape
    for j, step in enumerate((-1, 0, 1)):
        moved = value if step == 0 else shift_columns(value, step)
        padded[j, frame, 1 : rows + 1] = moved.astype(bf16)


def clear_edges(padded):
    rows = padded.shape[2]
    zero = jnp.zeros(padded.shape[:2] + padded.shape[3:], bf16)
    padded[:, :, 0] = zero
    padded[:, :, rows - 1] = zero


def hidden_of(value, mean, inv, gain, bias):
    affine = (value.astype(f32) - mean) * inv * gain + bias
    return affine * jax.nn.sigmoid(affine)


def tap_block(padded, frames, rows, t, i):
    width = padded.shape[-1]
    return [padded[j, t : t + frames, i : i + rows].reshape(-1, width) for j in range(KS)]


def groups_of_taps():
    return ((0, 1), (2,))


def weight_own_kernel(
    members,
    clip_ref, stats_ref, other_ref, gain_ref, bias_ref, cot_t_ref,
    padded, early_ref, late_ref,
):
    frames, rows, cols, width = clip_ref.shape
    mean, inv = moments(stats_ref, other_ref, members)
    clear_edges(padded)
    for frame in range(frames):
        place(padded, frame, hidden_of(clip_ref[frame], mean, inv, gain_ref[...], bias_ref[...]))
    per_frame = rows * cols
    for t in range(KT - 1, -1, -1):
        skipped = KT - 1 - t
        cot_t = cot_t_ref[:, skipped * per_frame :]
        base = row = t * KS * KS * width
        for group in groups_of_taps():
            parts = []
            for i in group:
                parts += tap_block(padded, frames - skipped, rows, 0, i)
            if t == KT - 1 and group[-1] == KS - 1:
                parts.append(clip_ref[...].reshape(-1, width))
            part = jnp.dot(cot_t, jnp.concatenate(parts, axis=1), preferred_element_type=f32)
            stop = row + part.shape[1]
            if t == KT - 1:
                late_ref[row - base : stop - base, :] = part.T
            else:
                early_ref[:, row:stop] = part
            row = stop


def weight_halo_kernel(
    members, split,
    halo_ref, clip_ref, stats_ref, other_ref, gain_ref, bias_ref, cot_t_ref, early_ref, late_ref,
    padded, total, *rest,
):
    at_start = lax.axis_index("ctx") == 0
    lead, rows, cols, width = halo_ref.shape
    mean, inv = moments(stats_ref, other_ref, members)
    clear_edges(padded)
    for frame in range(lead):
        value = jnp.where(at_start, clip_ref[0].astype(f32), halo_ref[frame].astype(f32))
        place(padded, frame, hidden_of(value, mean, inv, gain_ref[...], bias_ref[...]))
    per_frame = rows * cols

    def give(part, begin):
        if split is None:
            total[begin : begin + part.shape[0], :] = part
        else:
            scatter_rows(total, part, begin, split)

    give(late_ref[...], early_ref.shape[1])
    row = 0
    for t in range(KT - 1):
        count = lead - t
        for group in groups_of_taps():
            parts = []
            for i in group:
                parts += tap_block(padded, count, rows, t, i)
            part = jnp.dot(
                cot_t_ref[:, : count * per_frame], jnp.concatenate(parts, axis=1), preferred_element_type=f32
            )
            stop = row + part.shape[1]
            give((part + early_ref[:, row:stop]).T, row)
            row = stop
    if split is not None:
        (send_ref,) = rest
        core = lax.rem(lax.axis_index("dp"), 2)
        halves, blocks = send_ref.shape[:2]
        for half in range(halves):
            for k in range(blocks):
                send_ref[half, k] = total[half, 2 * k + 1 - core].astype(bf16)


def scatter_rows(total, part, begin, split):
    conv_rows, short_rows, conv_all = split
    halves = total.shape[0]
    row, stop = begin, begin + part.shape[0]
    width = total.shape[-1]
    while row < stop:
        if row < conv_all:
            block, offset = divmod(row, conv_rows)
            count = min(conv_rows - offset, stop - row, conv_all - row)
            target = offset
        else:
            block, offset = divmod(row - conv_all, short_rows)
            count = min(short_rows - offset, stop - row)
            target = conv_rows + offset
        for half in range(halves):
            total[half, block, target : target + count, :] = part[
                row - begin : row - begin + count, half * width : (half + 1) * width
            ]
        row += count


def forward_kernel(padded_lead, padded, clip_ref, weight_ref, short_ref, out_ref):
    frames, rows, cols, width = clip_ref.shape
    lead = padded_lead.shape[1]
    for frame in range(frames):
        parts = []
        for t in range(KT):
            source, at = (padded_lead, frame + t) if frame + t < lead else (padded, frame + t - lead)
            for i in range(KS):
                parts += tap_block(source, 1, rows, at, i)
        result = jnp.dot(jnp.concatenate(parts, axis=1), weight_ref[...], preferred_element_type=f32)
        result = result + jnp.dot(
            clip_ref[frame].reshape(-1, width), short_ref[...], preferred_element_type=f32
        )
        out_ref[frame] = result.astype(bf16).reshape(rows, cols, -1)


def back_weights(weight_ref, width, taps_t):
    bands = []
    for t in taps_t:
        bands.append(
            jnp.concatenate(
                [weight_ref[(t * KS * KS + q) * width : (t * KS * KS + q + 1) * width, :] for q in range(KS * KS)],
                axis=1,
            )
        )
    return jnp.concatenate(bands, axis=0) if len(bands) > 1 else bands[0]


def spatial_block(padded, frame, rows):
    out_width = padded.shape[-1]
    parts = []
    for i in range(KS):
        for j in range(KS):
            parts.append(padded[2 - j, frame, 2 - i : 2 - i + rows].reshape(-1, out_width))
    return jnp.concatenate(parts, axis=1)


def back_dot(block, weights):
    return lax.dot_general(block, weights, (((1,), (1,)), ((), ())), preferred_element_type=f32)


def back_products(begin, count, cot_ref, weight_ref, width, padded):
    rows, cols, out_width = cot_ref.shape[1:]
    clear_edges(padded)
    late = back_weights(weight_ref, width, (2, 1))
    early = back_weights(weight_ref, width, (0,))
    products = []
    for at in range(count):
        place(padded, at, cot_ref[begin + at].astype(f32))
        block = spatial_block(padded, at, rows)
        both = back_dot(block, late)
        products.append((both[:, :width], both[:, width:], back_dot(block, early)))
    return products


def back_first_kernel(cot_ref, weight_ref, out_ref, before_ref, cot_t_ref, padded):
    out_width = cot_ref.shape[-1]
    at_start = lax.axis_index("ctx") == 0
    cot_t_ref[...] = cot_ref[...].reshape(-1, out_width).T
    width = out_ref.shape[-1]
    (a2, a1, a0), (b2, b1, b0) = back_products(0, 2, cot_ref, weight_ref, width, padded)
    last = a1 + b0
    before_ref[0] = a0.astype(bf16)
    before_ref[1] = last.astype(bf16)
    out_ref[0] = a2 + b1 + jnp.where(at_start, a0 + last, 0.0)
    out_ref[1] = b2


def back_second_kernel(cot_ref, weight_ref, first_ref, out_ref, padded):
    width = out_ref.shape[-1]
    frames = cot_ref.shape[0]
    out_ref[0:2] = first_ref[...]
    for frame, (same, one, two) in enumerate(back_products(2, frames - 2, cot_ref, weight_ref, width, padded), 2):
        out_ref[frame] = same
        out_ref[frame - 1] += one
        out_ref[frame - 2] += two


def activation_kernel(
    members,
    part_ref, leading_ref, clip_ref, halo_ref, stats_ref, other_ref, gain_ref, bias_ref, forward_ref,
    grad_ref, slope_ref, sums_ref, out_ref, whole_ref, sem,
):
    copy = pltpu.make_async_copy(forward_ref, whole_ref, sem)
    copy.start()
    frames, rows, cols, width = clip_ref.shape
    places = rows * cols
    gain = gain_ref[...]
    mean, inv = moments(stats_ref, other_ref, members)

    def standard_and_slope(value):
        standard = (value.astype(f32) - mean) * inv
        affine = standard * gain + bias_ref[...]
        logistic = jax.nn.sigmoid(affine)
        return standard, logistic * (1.0 + affine * (1.0 - logistic)) * gain

    total = jnp.zeros((1, width), f32)
    cross = jnp.zeros((1, width), f32)
    lead = leading_ref.shape[0]
    for frame in range(lead):
        here = slice(frame * places, (frame + 1) * places)
        standard, slope = standard_and_slope(halo_ref[frame].reshape(-1, width))
        grad = leading_ref[frame].astype(f32) * slope
        total = total + column_totals(grad)
        cross = cross + column_totals(grad * standard)
        out_ref[here] = leading_ref[frame]
    at_start = lax.axis_index("ctx") == 0
    total = jnp.where(at_start, 0.0, total)
    cross = jnp.where(at_start, 0.0, cross)
    for frame in range(frames):
        standard, slope = standard_and_slope(clip_ref[frame].reshape(-1, width))
        grad = part_ref[frame] * slope
        grad_ref[frame] = grad
        if frame >= frames - lead:
            slope_ref[frame - (frames - lead)] = slope
        total = total + column_totals(grad)
        cross = cross + column_totals(grad * standard)
    sums = group_totals(two_rows(total, cross))
    sums_ref[...] = sums
    out_ref[lead * places :] = pieces_block(sums)
    copy.wait()


def finish_kernel(
    members,
    grad_ref, slope_ref, sums_ref, after_ref, clip_ref, stats_ref, other_ref, cot_ref, short_ref,
    out_ref,
):
    frames, rows, cols, width = clip_ref.shape
    places = rows * cols
    out_width = cot_ref.shape[-1]
    lead = slope_ref.shape[0]
    is_last = lax.axis_index("ctx") == lax.axis_size("ctx") - 1
    mean, inv = moments(stats_ref, other_ref, members)
    sums = sums_ref[0:2] + whole(after_ref)
    mean_grad = sums[0:1] / members
    mean_cross = sums[1:2] / members
    for frame in range(frames):
        standard = (clip_ref[frame].reshape(-1, width).astype(f32) - mean) * inv
        shortcut = back_dot(cot_ref[frame].reshape(-1, out_width), short_ref[...])
        grad = grad_ref[frame]
        at = frame - (frames - lead)
        if at >= 0:
            following = after_ref[at * places : (at + 1) * places].astype(f32) * slope_ref[at]
            grad = grad + jnp.where(is_last, 0.0, following)
        grad = (grad - mean_grad - standard * mean_cross) * inv + shortcut
        out_ref[frame] = grad.astype(bf16).reshape(rows, cols, width)


def first_kernel(total_ref, got_ref, keep_ref, *send_refs):
    at = lax.axis_index("dp")
    z, x, core = at // 4, lax.rem(at // 2, 2), lax.rem(at, 2)
    y = lax.axis_index("ctx")
    plane = x + 2 * y
    for step, target in enumerate((keep_ref, *send_refs)):
        for inner in range(4):
            to_plane = jnp.where(core == 0, lax.bitwise_xor(plane, step), inner)
            to_z = jnp.where(core == 0, inner, lax.bitwise_xor(z, step))
            to_x, to_y = lax.rem(to_plane, 2), to_plane // 2
            value = total_ref[to_y, to_z, to_x, core] + got_ref[to_y, to_z, to_x].astype(f32)
            target[inner] = value.astype(target.dtype)


def second_kernel(keep_ref, a_ref, b_ref, c_ref, own_ref, *send_refs):
    at = lax.axis_index("dp")
    plane = lax.rem(at // 2, 2) + 2 * lax.axis_index("ctx")
    here = jnp.where(lax.rem(at, 2) == 0, at // 4, plane)
    for step, target in enumerate((own_ref, *send_refs)):
        to = lax.bitwise_xor(here, step)
        value = keep_ref[to] + a_ref[to].astype(f32) + (b_ref[to].astype(f32) + c_ref[to].astype(f32))
        target[...] = value.astype(target.dtype)


def last_kernel(scale, own_ref, a_ref, b_ref, c_ref, conv_ref, short_ref):
    value = own_ref[...] + a_ref[...].astype(f32) + (b_ref[...].astype(f32) + c_ref[...].astype(f32))
    value = value * scale
    conv_ref[...] = value[: conv_ref.shape[0]]
    short_ref[...] = value[conv_ref.shape[0] :]


def from_behind(value, axis, steps):
    count = lax.axis_size(axis)
    initial, last = (max(0, -steps), min(count, count - steps))
    return lax.ppermute(value, axis, [(source, source + steps) for source in range(initial, last)])


def others_total(value):
    count = lax.axis_size("ctx")
    total = None
    for step in range(1, count):
        got = lax.ppermute(value, "ctx", [(source, (source + step) % count) for source in range(count)])
        total = got if total is None else total + got
    return jnp.zeros_like(value) if total is None else total


def swap(value, core_0, core_1):
    dp, ctx = lax.axis_size("dp"), lax.axis_size("ctx")
    masks = (core_0, core_1)
    pairs = []
    for source in range(dp * ctx):
        at, side = divmod(source, ctx)
        dp_mask, ctx_mask = masks[at % 2]
        pairs.append((source, (at ^ dp_mask) * ctx + (side ^ ctx_mask)))
    return lax.ppermute(value, ("dp", "ctx"), pairs)


def exchange(sends, plane_core):
    got = []
    for step in (3, 2, 1):
        masks = [None, None]
        masks[plane_core] = (2 * (step % 2), step // 2)
        masks[1 - plane_core] = (4 * step, 0)
        got.append(swap(sends[step - 1], *masks))
    return got


def sort_first(total, got):
    halves, blocks, rows, cols = got.shape
    part = (4, rows, cols)
    return call(
        first_kernel,
        [jax.ShapeDtypeStruct(part, f32)] + [jax.ShapeDtypeStruct(part, bf16)] * 3,
    )(total.reshape(halves, blocks // 2, 2, 2, rows, cols), got.reshape(halves, blocks // 2, 2, rows, cols))


def sort_second(keep, *got):
    part = keep.shape[1:]
    return call(
        second_kernel,
        [jax.ShapeDtypeStruct(part, f32)] + [jax.ShapeDtypeStruct(part, bf16)] * 3,
    )(keep, *got)


def add_last(mine, from_a, from_b, from_c, conv_rows, short_rows, scale):
    cols = mine.shape[1]
    return call(
        functools.partial(last_kernel, scale),
        [jax.ShapeDtypeStruct((conv_rows, cols), f32), jax.ShapeDtypeStruct((short_rows, cols), f32)],
        moved=mine.size * 12,
    )(mine, from_a, from_b, from_c)


def body(clip_in, norm_gain, norm_bias, conv_weight, short_weight, out_cotangent):
    batch_clips, frames, height, breadth, in_width = clip_in.shape
    assert batch_clips == 1
    out_width = conv_weight.shape[1]
    per_group = in_width // GROUPS
    dp_size, ctx_size = lax.axis_size("dp"), lax.axis_size("ctx")
    total_frames = frames * ctx_size
    members = total_frames * height * breadth * per_group
    scale = 1.0 / (batch_clips * dp_size * total_frames)
    places = frames * height * breadth
    clip = clip_in[0]
    cot = out_cotangent[0]
    gain = norm_gain.reshape(1, in_width)
    bias = norm_bias.reshape(1, in_width)
    conv_all = TAPS * in_width
    work = places * conv_all * out_width * 2

    lead = KT - 1
    stats, last_clip = call(
        start_kernel,
        [jax.ShapeDtypeStruct((8, in_width), f32), jax.ShapeDtypeStruct((lead,) + clip.shape[1:], bf16)],
        flops=work, moved=clip.size * 2,
    )(clip)
    other = others_total(stats)
    halo = from_behind(last_clip, "ctx", 1)

    half_cot = pltpu.VMEM((KS, 2, height + 2, breadth, out_width), bf16)
    first_part, leading, cot_t = call(
        back_first_kernel,
        [
            jax.ShapeDtypeStruct((2, height * breadth, in_width), f32),
            jax.ShapeDtypeStruct((lead, height * breadth, in_width), bf16),
            jax.ShapeDtypeStruct((out_width, places), bf16),
        ],
        [half_cot],
        flops=work, moved=conv_weight.size * 2,
    )(cot, conv_weight)
    padded = (KS, frames, height + 2, breadth, in_width)
    late_at = (KT - 1) * KS * KS * in_width
    hidden, early, late = call(
        functools.partial(weight_own_kernel, members),
        [
            jax.ShapeDtypeStruct(padded, bf16),
            jax.ShapeDtypeStruct((out_width, late_at), f32),
            jax.ShapeDtypeStruct((conv_all + in_width - late_at, out_width), f32),
        ],
        flops=work, moved=cot.size * 2,
    )(clip, stats, other, gain, bias, cot_t)

    staged = dp_size == 16 and ctx_size == 2
    conv_rows, short_rows = conv_all // dp_size, in_width // dp_size
    if staged:
        cols = out_width // ctx_size
        block = (conv_rows + short_rows, cols)
        outs = [
            jax.ShapeDtypeStruct((ctx_size, dp_size) + block, f32),
            jax.ShapeDtypeStruct((ctx_size, dp_size // 2) + block, bf16),
        ]
        split = (conv_rows, short_rows, conv_all)
    else:
        outs = [jax.ShapeDtypeStruct((conv_all + in_width, out_width), f32)]
        split = None
    hidden_lead, *parts = call(
        functools.partial(weight_halo_kernel, members, split),
        [jax.ShapeDtypeStruct((KS, lead) + padded[2:], bf16)] + outs,
        flops=work // 3, moved=cot.size * 2,
    )(halo, clip, stats, other, gain, bias, cot_t, early, late)

    first_part, hidden_lead = lax.optimization_barrier((first_part, hidden_lead))
    back_part = call(
        back_second_kernel,
        jax.ShapeDtypeStruct((frames, height * breadth, in_width), f32),
        [half_cot],
        flops=work // 4,
    )(cot, conv_weight, first_part)
    if staged:
        got, back_part = lax.optimization_barrier((swap(parts[1], (1, 0), (1, 0)), back_part))
        keep, *sends = sort_first(parts[0], got)
        got = exchange(sends, 0)
        hidden, keep = lax.optimization_barrier((hidden, keep))
    forward = call(
        forward_kernel,
        jax.ShapeDtypeStruct((frames, height, breadth, out_width), bf16),
        flops=work // 4,
    )(hidden_lead, hidden, clip, conv_weight, short_weight)
    anywhere, vmem = pl.BlockSpec(memory_space=pl.ANY), pl.BlockSpec(memory_space=pltpu.VMEM)
    grad, slope, sums, parcel, clip_out = call(
        functools.partial(activation_kernel, members),
        [
            jax.ShapeDtypeStruct((frames, height * breadth, in_width), f32),
            jax.ShapeDtypeStruct((lead, height * breadth, in_width), f32),
            jax.ShapeDtypeStruct((8, in_width), f32),
            jax.ShapeDtypeStruct((lead * height * breadth + 16, in_width), bf16),
            jax.ShapeDtypeStruct(forward.shape, bf16),
        ],
        [pltpu.SemaphoreType.DMA],
        in_specs=[vmem] * 9,
        out_specs=[vmem] * 4 + [anywhere],
    )(back_part, leading, clip, halo, stats, other, gain, bias, forward)
    if ctx_size == 2:
        after = lax.ppermute(parcel, "ctx", [(0, 1), (1, 0)])
    else:
        after = from_behind(leading, "ctx", -1).reshape(-1, in_width)
        after = jnp.concatenate([after, pieces_block(others_total(sums))], axis=0)
    if staged:
        *got, sums = lax.optimization_barrier((*got, sums))
        mine, *sends = sort_second(keep, *got)
        got = exchange(sends, 1)
        conv_grad, short_grad = add_last(mine, *got, conv_rows, short_rows, scale)
        after, mine = lax.optimization_barrier((after, mine))
    else:
        summed = []
        for part in (parts[0][:conv_all], parts[0][conv_all:]):
            part = lax.psum_scatter(part, "dp", scatter_dimension=0, tiled=True)
            part = lax.psum_scatter(part, "ctx", scatter_dimension=1, tiled=True)
            summed.append(part * scale)
        conv_grad, short_grad = summed
    clip_grad = call(
        functools.partial(finish_kernel, members),
        jax.ShapeDtypeStruct((frames, height, breadth, in_width), bf16),
        flops=work // 20, moved=cot.size * 4,
    )(grad, slope, sums, after, clip, stats, other, cot, short_weight)
    return (clip_out[None], clip_grad[None], conv_grad, short_grad)


def solution(mesh):
    return jax.shard_map(
        body,
        mesh=mesh,
        in_specs=(
            P("dp", "ctx", None, None, None),
            P(),
            P(),
            P(),
            P(),
            P("dp", "ctx", None, None, None),
        ),
        out_specs=(
            P("dp", "ctx", None, None, None),
            P("dp", "ctx", None, None, None),
            P("dp", "ctx"),
            P("dp", "ctx"),
        ),
        check_vma=False,
    )
```
